32 devices in a mesh: dp: 2 (over y), seq: 16 (over z, x, core).
Axes of the slice: x: 2, y: 2, z: 4, core: 2. Of those that a mesh axis runs over, the one named last changes fastest.
Arguments:
- signal: bfloat16 [8, 4, 512, 512], P(None, 'dp', 'seq'), may hold values from -6 to 6
- cotangent: bfloat16 [8, 4, 512, 512], P(None, 'dp', 'seq'), may hold values from -6 to 6
- filter_spec: bfloat16 [2, 8, 512, 512], P(None, None, 'seq'), may hold values from -4.1875 to 4.1875
Outputs:
- output: bfloat16 [8, 4, 512, 512], P(None, 'dp', 'seq')
- grad_signal: bfloat16 [8, 4, 512, 512], P(None, 'dp', 'seq')
- grad_filter: bfloat16 [2, 8, 512, 512], P(None, None, 'seq')
The draws below stay inside these ranges and needn't reach their ends.
All inputs are finite; a program needn't handle non-finite values.
Results may differ from the reference program's by a relative error of at most 0.0091.
Values may be sent and summed in bfloat16 or wider, within the bound.
A program may use at most 64 MiB of HBM per device.

```python
import math
import jax
import jax.numpy as jnp
from jax import lax

NB = 512
NR = 512
FILT = 8
GSIZE = 4


def shard_levels(rng, shape, pieces, smallest, high):
    level = 1.0
    for dim, shards_of in pieces:
        heights = jax.random.uniform(jax.random.fold_in(jax.random.fold_in(rng, 6), dim), (shards_of,), jnp.float32, smallest / len(pieces), high / len(pieces))
        level = level * jnp.repeat(jnp.exp(heights), shape[dim] // shards_of).reshape((-1,) + (1,) * (len(shape) - 1 - dim))
    return level


def centred(rng, dims, spread, reach, cuts=(), kind=jnp.bfloat16):
    entries = jax.random.normal(rng, dims, jnp.float32) * spread
    if len(cuts) > 0:
        entries = shard_levels(rng, dims, cuts, -0.22, 0.18) * entries
    return jnp.clip(entries, min=-reach, max=reach).astype(kind)


def setup_inputs(seed: int = 0) -> dict:
    arg_keys = jax.random.split(jax.random.key(seed), 4)
    signal = centred(arg_keys[0], (FILT, GSIZE, NR, NB), 1.0, 6.0, ((1, 2), (2, 16)))
    cotangent = centred(arg_keys[1], (FILT, GSIZE, NR, NB), 1.0, 6.0, ((1, 2), (2, 16)))
    filter_spec = centred(arg_keys[2], (2, FILT, NB, NR), 0.7, 4.1875, ((2, 16),))
    return {"signal": signal, "cotangent": cotangent, "filter_spec": filter_spec}


def unit_tables(block_size):
    steps_index = jnp.arange(block_size, dtype=jnp.int32)
    product_index = steps_index[:, None] * steps_index[None, :] % block_size
    phases = product_index.astype(jnp.float32) * (2.0 * math.pi / block_size)
    factor = 1.0 / math.sqrt(block_size)
    return ((jnp.cos(phases) * factor).astype(jnp.bfloat16), (-jnp.sin(phases) * factor).astype(jnp.bfloat16))

def twiddle(row_index, col_index, length_all, orient):
    phases = (row_index[:, None] * col_index[None, :]).astype(jnp.float32) * (orient * 2.0 * math.pi / length_all)
    return (jnp.cos(phases), jnp.sin(phases))

def rounded(values):
    return lax.optimization_barrier(values.astype(jnp.bfloat16)).astype(jnp.float32)

def contract(first_operand, second_operand, pattern):
    return jnp.einsum(pattern, first_operand, second_operand, precision=lax.Precision.HIGHEST)

def spectrum(signal_one, big_cos, big_sin, small_cos, small_sin, turn_cos, turn_sin):
    signal_wide = signal_one.astype(jnp.float32)
    real_part = contract(signal_wide, big_cos, 'crs,as->cra')
    imaginary = contract(signal_wide, big_sin, 'crs,as->cra')
    mid_real = rounded(real_part * turn_cos - imaginary * turn_sin)
    mid_imaginary = rounded(real_part * turn_sin + imaginary * turn_cos)
    out_real = contract(mid_real, small_cos, 'cra,qr->caq') - contract(mid_imaginary, small_sin, 'cra,qr->caq')
    out_imaginary = contract(mid_imaginary, small_cos, 'cra,qr->caq') + contract(mid_real, small_sin, 'cra,qr->caq')
    return (out_real, out_imaginary)

def restore(spec_real, spec_imaginary, big_cos, big_sin, small_cos, small_sin, turn_cos, turn_sin):
    real_part = contract(spec_real, small_cos, 'caq,rq->car') + contract(spec_imaginary, small_sin, 'caq,rq->car')
    imaginary = contract(spec_imaginary, small_cos, 'caq,rq->car') - contract(spec_real, small_sin, 'caq,rq->car')
    mid_real = rounded(real_part * turn_cos - imaginary * turn_sin)
    mid_imaginary = rounded(real_part * turn_sin + imaginary * turn_cos)
    total = contract(mid_real, big_cos, 'car,sa->crs') + contract(mid_imaginary, big_sin, 'car,sa->crs')
    return total.astype(jnp.bfloat16)

def reference(signal, cotangent, filter_spec):
    big_table_cos, big_table_sin = unit_tables(NB)
    small_table_cos, small_table_sin = unit_tables(NR)
    big_cos = big_table_cos.astype(jnp.float32)
    big_sin = big_table_sin.astype(jnp.float32)
    small_cos = small_table_cos.astype(jnp.float32)
    small_sin = small_table_sin.astype(jnp.float32)
    freq_index = jnp.arange(NB, dtype=jnp.int32)
    row_index = jnp.arange(NR, dtype=jnp.int32)
    fwd_cos, fwd_sin = twiddle(row_index, freq_index, NB * NR, -1.0)
    inv_cos, inv_sin = twiddle(freq_index, row_index, NB * NR, 1.0)
    filter_reals = filter_spec[0].astype(jnp.float32)
    filter_imags = filter_spec[1].astype(jnp.float32)

    def group_step(carried, inputs):
        signal_one, cotangent_one, filter_real, filter_imaginary = inputs
        sig_real, sig_imaginary = spectrum(signal_one, big_cos, big_sin, small_cos, small_sin, fwd_cos, fwd_sin)
        cot_real, cot_imaginary = spectrum(cotangent_one, big_cos, big_sin, small_cos, small_sin, fwd_cos, fwd_sin)
        filter_real = filter_real[None]
        filter_imaginary = filter_imaginary[None]
        prod_real = rounded(filter_real * sig_real - filter_imaginary * sig_imaginary)
        prod_imaginary = rounded(filter_real * sig_imaginary + filter_imaginary * sig_real)
        back_real = rounded(filter_real * cot_real + filter_imaginary * cot_imaginary)
        back_imaginary = rounded(filter_real * cot_imaginary - filter_imaginary * cot_real)
        output_one = restore(prod_real, prod_imaginary, big_cos, big_sin, small_cos, small_sin, inv_cos, inv_sin)
        grad_one = restore(back_real, back_imaginary, big_cos, big_sin, small_cos, small_sin, inv_cos, inv_sin)
        grad_terms = jnp.stack([lax.optimization_barrier(jnp.sum(cot_real * sig_real + cot_imaginary * sig_imaginary, axis=0)), lax.optimization_barrier(jnp.sum(cot_imaginary * sig_real - cot_real * sig_imaginary, axis=0))])
        return (carried, (output_one, grad_one, grad_terms.astype(jnp.bfloat16)))
    initial = jnp.zeros((), jnp.float32)
    unused, (output, grad_signal, grad_groups) = lax.scan(group_step, initial, (signal, cotangent, filter_reals, filter_imags))
    grad_filter = jnp.transpose(grad_groups, (1, 0, 2, 3))
    return (output, grad_signal, grad_filter)
```

```python
import functools
import math

import jax
import jax.numpy as jnp
import numpy as np
from jax import lax
from jax.experimental import pallas as pl
from jax.experimental.pallas import tpu as pltpu
from jax.sharding import PartitionSpec as P

MESH = pl.DeviceIdType.MESH

NB = 512


def unit_tables(block_size):
    steps_index = jnp.arange(block_size, dtype=jnp.int32)
    product_index = steps_index[:, None] * steps_index[None, :] % block_size
    phases = product_index.astype(jnp.float32) * (2.0 * math.pi / block_size)
    factor = 1.0 / math.sqrt(block_size)
    return (
        (jnp.cos(phases) * factor).astype(jnp.bfloat16),
        (-jnp.sin(phases) * factor).astype(jnp.bfloat16),
    )


def twiddle(row_index, col_index, length_all, orient):
    phases = (row_index[:, None] * col_index[None, :]).astype(jnp.float32) * (
        orient * 2.0 * math.pi / length_all
    )
    return (jnp.cos(phases), jnp.sin(phases))


def forward_rows(signal, tables, first_row, length_all):
    big_cos, big_sin, small_cos, small_sin = tables
    real_part = jnp.einsum("ncrs,as->ncra", signal, big_cos, preferred_element_type=jnp.float32)
    imaginary = jnp.einsum("ncrs,as->ncra", signal, big_sin, preferred_element_type=jnp.float32)
    row_index = first_row + jnp.arange(signal.shape[2], dtype=jnp.int32)
    col_index = jnp.arange(signal.shape[3], dtype=jnp.int32)
    turn_cos, turn_sin = twiddle(row_index, col_index, length_all, -1.0)
    middle = jnp.stack(
        [real_part * turn_cos - imaginary * turn_sin, real_part * turn_sin + imaginary * turn_cos]
    ).astype(jnp.bfloat16)
    received = lax.all_to_all(middle, "seq", split_axis=4, concat_axis=3, tiled=True)
    real_received = received[0]
    imaginary_received = received[1]
    out_real = jnp.einsum(
        "ncra,qr->ncaq", real_received, small_cos, preferred_element_type=jnp.float32
    ) - jnp.einsum(
        "ncra,qr->ncaq", imaginary_received, small_sin, preferred_element_type=jnp.float32
    )
    out_imaginary = jnp.einsum(
        "ncra,qr->ncaq", imaginary_received, small_cos, preferred_element_type=jnp.float32
    ) + jnp.einsum("ncra,qr->ncaq", real_received, small_sin, preferred_element_type=jnp.float32)
    return jnp.stack([out_real, out_imaginary])


def inverse_rows(spectrum, tables, first_freq, length_all):
    big_cos, big_sin, small_cos, small_sin = tables
    real_part = jnp.einsum(
        "ncaq,rq->ncar", spectrum[0], small_cos, preferred_element_type=jnp.float32
    ) + jnp.einsum("ncaq,rq->ncar", spectrum[1], small_sin, preferred_element_type=jnp.float32)
    imaginary = jnp.einsum(
        "ncaq,rq->ncar", spectrum[1], small_cos, preferred_element_type=jnp.float32
    ) - jnp.einsum("ncaq,rq->ncar", spectrum[0], small_sin, preferred_element_type=jnp.float32)
    row_index = first_freq + jnp.arange(spectrum.shape[3], dtype=jnp.int32)
    col_index = jnp.arange(spectrum.shape[4], dtype=jnp.int32)
    turn_cos, turn_sin = twiddle(row_index, col_index, length_all, 1.0)
    middle = jnp.stack(
        [real_part * turn_cos - imaginary * turn_sin, real_part * turn_sin + imaginary * turn_cos]
    ).astype(jnp.bfloat16)
    received = lax.all_to_all(middle, "seq", split_axis=4, concat_axis=3, tiled=True)
    total = jnp.einsum(
        "ncar,sa->ncrs", received[0], big_cos, preferred_element_type=jnp.float32
    ) + jnp.einsum("ncar,sa->ncrs", received[1], big_sin, preferred_element_type=jnp.float32)
    return total.astype(jnp.bfloat16)


def body(signal, cotangent, filter_spec):
    rows_total = signal.shape[2] * lax.axis_size("seq")
    big_cos, big_sin = unit_tables(NB)
    small_cos, small_sin = unit_tables(rows_total)
    tables = (big_cos, big_sin, small_cos, small_sin)
    length_all = NB * rows_total
    first_row = lax.axis_index("seq") * signal.shape[2]
    first_freq = lax.axis_index("seq") * (NB // lax.axis_size("seq"))
    filter_real = filter_spec[0].astype(jnp.float32)[:, None]
    filter_imaginary = filter_spec[1].astype(jnp.float32)[:, None]
    channels = signal.shape[1]
    stacked = forward_rows(
        jnp.concatenate([signal, cotangent], axis=1), tables, first_row, length_all
    )
    signal_spec = stacked[:, :, :channels]
    cotangent_spec = stacked[:, :, channels:]
    joined_input = jnp.concatenate(
        [
            jnp.stack(
                [
                    filter_real * signal_spec[0] - filter_imaginary * signal_spec[1],
                    filter_real * signal_spec[1] + filter_imaginary * signal_spec[0],
                ]
            ).astype(jnp.bfloat16),
            jnp.stack(
                [
                    filter_real * cotangent_spec[0] + filter_imaginary * cotangent_spec[1],
                    filter_real * cotangent_spec[1] - filter_imaginary * cotangent_spec[0],
                ]
            ).astype(jnp.bfloat16),
        ],
        axis=2,
    )
    results = inverse_rows(joined_input, tables, first_freq, length_all)
    output = results[:, :channels]
    grad_signal = results[:, channels:]
    grad_terms = jnp.stack(
        [
            jnp.sum(
                cotangent_spec[0] * signal_spec[0] + cotangent_spec[1] * signal_spec[1], axis=1
            ),
            jnp.sum(
                cotangent_spec[1] * signal_spec[0] - cotangent_spec[0] * signal_spec[1], axis=1
            ),
        ]
    )
    grad_filter = lax.psum(grad_terms, "dp")
    return (output, grad_signal, grad_filter.astype(jnp.bfloat16))


def whole_tables(size):
    index = np.arange(size)
    phases = (index[:, None] * index[None, :] % size) * (2.0 * math.pi / size)
    factor = 1.0 / math.sqrt(size)
    cos_table, sin_table = np.cos(phases) * factor, -np.sin(phases) * factor
    forward = np.block([[cos_table, sin_table], [-sin_table, cos_table]])
    turn = (index[:, None] * index[None, :]) * (2.0 * math.pi / (size * size))
    return (
        forward.astype(jnp.bfloat16),
        forward.T.astype(jnp.bfloat16),
        np.cos(turn).astype(np.float32),
        np.sin(turn).astype(np.float32),
    )


def whole_sequences_fit(mesh, signal, filter_spec):
    filters, channels, rows, size = signal.shape
    n = mesh.shape["seq"]
    return (
        mesh.shape["dp"] == 2
        and channels == 2
        and filters * channels == n
        and rows * n == size
        and filter_spec.shape[2] == rows
        and filter_spec.shape[3] == size
        and rows % 32 == 0
        and size % 256 == 0
    )


def whole_kernel(
    n,
    signal_ref,
    cotangent_ref,
    filter_ref,
    forward_ref,
    inverse_ref,
    cos_ref,
    sin_ref,
    output_ref,
    grad_signal_ref,
    grad_filter_ref,
    signal_all,
    cotangent_all,
    filter_all,
    forward_table,
    inverse_table,
    turn_cos,
    turn_sin,
    signal_spec,
    cotangent_spec,
    middle,
    output_all,
    grad_all,
    terms_wide,
    terms,
    terms_got,
    grad_part,
    table_sem,
    filter_send,
    filter_got,
    share_send,
    share_got,
    signal_send,
    signal_got,
    cotangent_send,
    cotangent_got,
    output_send,
    output_got,
    grad_send,
    grad_got,
    terms_send,
    terms_recv,
    part_send,
    part_got,
    swap_send,
    swap_got,
):
    size = signal_all.shape[0]
    rows = size // n
    half = rows // 2
    chunk = 256
    chunks = size // chunk
    per_chunk = chunk // rows
    me = lax.axis_index("seq")
    side = lax.axis_index("dp")
    other = 1 - side
    channel = lax.rem(me, 2)
    group = lax.div(me, 2)
    mate = me + 1 - 2 * channel
    my_half = pl.ds(pl.multiple_of(channel * half, half), half)
    my_rows = pl.ds(pl.multiple_of(me * rows, rows), rows)
    partners = ((side, mate), (other, me), (other, mate))

    table_copies = [
        pltpu.make_async_copy(source, target, table_sem.at[i])
        for i, (source, target) in enumerate(
            (
                (forward_ref, forward_table),
                (inverse_ref, inverse_table),
                (cos_ref, turn_cos),
                (sin_ref, turn_sin),
            )
        )
    ]
    for copy in table_copies:
        copy.start()

    barrier = pltpu.get_barrier_semaphore()

    def greet(k, carry):
        pl.semaphore_signal(
            barrier, inc=1, device_id={"dp": side, "seq": lax.rem(me + k, n)}, device_id_type=MESH
        )
        return carry

    lax.fori_loop(1, n, greet, 0)
    for to_side, to_seq in partners[1:]:
        pl.semaphore_signal(
            barrier, inc=1, device_id={"dp": to_side, "seq": to_seq}, device_id_type=MESH
        )
    pl.semaphore_wait(barrier, n + 1)

    def send_all(source_of, target, send_sem, recv_sem):
        pltpu.make_async_copy(source_of(me), target, recv_sem).start()

        def one(k, carry):
            to = lax.rem(me + k, n)
            pltpu.make_async_remote_copy(
                src_ref=source_of(to),
                dst_ref=target,
                send_sem=send_sem,
                recv_sem=recv_sem,
                device_id={"dp": side, "seq": to},
                device_id_type=MESH,
            ).start()
            return carry

        lax.fori_loop(1, n, one, 0)

    def wait_bytes(ref, sem):
        pltpu.make_async_copy(ref, ref, sem).wait()

    def filter_source(to):
        start = pl.multiple_of(lax.rem(to, 2) * half, half)
        return filter_ref.at[side, lax.div(to, 2), pl.ds(start, half), :]

    pltpu.make_async_copy(
        filter_source(me), filter_all.at[side, me, my_half, :], filter_got
    ).start()

    def send_filter(k, carry):
        to = lax.rem(me + k, n)
        start = pl.multiple_of(lax.rem(to, 2) * half, half)
        pltpu.make_async_remote_copy(
            src_ref=filter_source(to),
            dst_ref=filter_all.at[side, me, pl.ds(start, half), :],
            send_sem=filter_send,
            recv_sem=filter_got,
            device_id={"dp": side, "seq": to},
            device_id_type=MESH,
        ).start()
        return carry

    lax.fori_loop(1, n, send_filter, 0)
    send_all(
        lambda to: signal_ref.at[lax.div(to, 2), lax.rem(to, 2)],
        signal_all.at[my_rows, :],
        signal_send,
        signal_got,
    )
    send_all(
        lambda to: cotangent_ref.at[lax.div(to, 2), lax.rem(to, 2)],
        cotangent_all.at[my_rows, :],
        cotangent_send,
        cotangent_got,
    )

    my_quarter = filter_all.at[side, :, my_half, :]
    wait_bytes(my_quarter, filter_got)
    share_copies = [
        pltpu.make_async_remote_copy(
            src_ref=my_quarter,
            dst_ref=my_quarter,
            send_sem=share_send.at[i],
            recv_sem=share_got.at[i],
            device_id={"dp": to_side, "seq": to_seq},
            device_id_type=MESH,
        )
        for i, (to_side, to_seq) in enumerate(partners)
    ]
    for copy in share_copies:
        copy.start()

    for copy in table_copies:
        copy.wait()

    def transform(values, spec, i):
        at = pl.ds(pl.multiple_of(i * chunk, chunk), chunk)
        one_signal = values[...]
        contract_last = (((1,), (1,)), ((), ()))
        real = lax.dot_general(
            forward_table[at, :size], one_signal, contract_last, preferred_element_type=jnp.float32
        )
        imaginary = lax.dot_general(
            forward_table[at, size:], one_signal, contract_last, preferred_element_type=jnp.float32
        )
        cos_part, sin_part = turn_cos[at, :], turn_sin[at, :]
        mid = jnp.concatenate(
            [
                (real * cos_part + imaginary * sin_part).astype(jnp.bfloat16),
                (imaginary * cos_part - real * sin_part).astype(jnp.bfloat16),
            ],
            axis=1,
        )
        spec[at, :] = jnp.dot(mid, forward_table[...], preferred_element_type=jnp.float32)

    def filtered(spec, sign, i):
        at = pl.ds(pl.multiple_of(i * chunk, chunk), chunk)
        blocks = pl.ds(i * per_chunk, per_chunk)
        filter_real = filter_all[0, blocks].reshape(chunk, size).astype(jnp.float32)
        filter_imaginary = filter_all[1, blocks].reshape(chunk, size).astype(jnp.float32) * sign
        real, imaginary = spec[at, :size], spec[at, size:]
        product = jnp.concatenate(
            [
                (filter_real * real - filter_imaginary * imaginary).astype(jnp.bfloat16),
                (filter_real * imaginary + filter_imaginary * real).astype(jnp.bfloat16),
            ],
            axis=1,
        )
        both = jnp.dot(product, inverse_table[...], preferred_element_type=jnp.float32)
        real, imaginary = both[:, :size], both[:, size:]
        cos_part, sin_part = turn_cos[at, :], turn_sin[at, :]
        middle[at, :] = (real * cos_part - imaginary * sin_part).astype(jnp.bfloat16)
        below = pl.ds(pl.multiple_of(size + i * chunk, chunk), chunk)
        middle[below, :] = (real * sin_part + imaginary * cos_part).astype(jnp.bfloat16)

    def restored(result, i):
        at = pl.ds(pl.multiple_of(i * chunk, chunk), chunk)
        turned = jnp.dot(
            forward_table[at, :], middle[...], preferred_element_type=jnp.float32
        )
        result[:, at] = turned.T.astype(jnp.bfloat16)

    def loop(fn):
        def one(i, carry):
            fn(i)
            return carry

        lax.fori_loop(0, chunks, one, 0)

    def rows_of(ref, to):
        return ref.at[pl.ds(pl.multiple_of(to * rows, rows), rows), :]

    wait_bytes(signal_all, signal_got)
    loop(lambda i: transform(signal_all, signal_spec, i))
    for copy in share_copies:
        copy.wait()
    loop(lambda i: filtered(signal_spec, 1.0, i))
    loop(lambda i: restored(output_all, i))
    send_all(
        lambda to: rows_of(output_all, to), output_ref.at[group, channel], output_send, output_got
    )

    wait_bytes(cotangent_all, cotangent_got)

    def transform_and_terms(i):
        transform(cotangent_all, cotangent_spec, i)
        at = pl.ds(pl.multiple_of(i * chunk, chunk), chunk)
        blocks = pl.ds(i * per_chunk, per_chunk)
        real, imaginary = signal_spec[at, :size], signal_spec[at, size:]
        back_real, back_imaginary = cotangent_spec[at, :size], cotangent_spec[at, size:]
        for part, values in enumerate(
            (
                back_real * real + back_imaginary * imaginary,
                back_imaginary * real - back_real * imaginary,
            )
        ):
            values = values.reshape(per_chunk, rows, size)
            terms_wide[part, blocks] = values
            terms[part, blocks] = values.astype(jnp.bfloat16)

    loop(transform_and_terms)
    terms_copies = []
    for i, (to_side, to_seq) in enumerate(partners):
        start = pl.multiple_of(lax.rem(to_seq, 2) * half, half)
        terms_copies.append(
            pltpu.make_async_remote_copy(
                src_ref=terms.at[to_side, :, pl.ds(start, half), :],
                dst_ref=terms_got.at[i],
                send_sem=terms_send.at[i],
                recv_sem=terms_recv.at[i],
                device_id={"dp": to_side, "seq": to_seq},
                device_id_type=MESH,
            )
        )
    for copy in terms_copies:
        copy.start()

    loop(lambda i: filtered(cotangent_spec, -1.0, i))
    loop(lambda i: restored(grad_all, i))
    send_all(
        lambda to: rows_of(grad_all, to), grad_signal_ref.at[group, channel], grad_send, grad_got
    )

    for copy in terms_copies:
        copy.wait()
    total = terms_wide[side, :, my_half, :]
    for i in range(3):
        total = total + terms_got[i].astype(jnp.float32)
    grad_part[...] = total.astype(jnp.bfloat16)
    send_all(
        lambda to: grad_part.at[to],
        grad_filter_ref.at[side, group, my_half, :],
        part_send,
        part_got,
    )
    wait_bytes(grad_filter_ref.at[side], part_got)
    swap = pltpu.make_async_remote_copy(
        src_ref=grad_filter_ref.at[side],
        dst_ref=grad_filter_ref.at[side],
        send_sem=swap_send,
        recv_sem=swap_got,
        device_id={"dp": other, "seq": me},
        device_id_type=MESH,
    )
    swap.start()

    wait_bytes(output_ref, output_got)
    wait_bytes(grad_signal_ref, grad_got)
    swap.wait()
    sent = pl.ds(0, size - rows)
    wait_bytes(signal_all.at[sent, :], signal_send)
    wait_bytes(cotangent_all.at[sent, :], cotangent_send)
    wait_bytes(output_all.at[sent, :], output_send)
    wait_bytes(grad_all.at[sent, :], grad_send)
    wait_bytes(grad_part.at[pl.ds(0, n - 1)], filter_send)
    wait_bytes(grad_part.at[pl.ds(0, n - 1)], part_send)


def whole_body(n, signal, cotangent, filter_spec):
    size = signal.shape[3]
    rows = signal.shape[2]
    half = rows // 2
    tables = [jnp.asarray(table) for table in whole_tables(size)]
    bf16, f32 = jnp.bfloat16, jnp.float32
    anywhere = pl.BlockSpec(memory_space=pl.ANY)
    one_sem = pltpu.SemaphoreType.DMA(())
    three = pltpu.SemaphoreType.DMA((3,))
    return pl.pallas_call(
        functools.partial(whole_kernel, n),
        out_shape=tuple(
            jax.ShapeDtypeStruct(x.shape, x.dtype) for x in (signal, cotangent, filter_spec)
        ),
        in_specs=[anywhere] * 7,
        out_specs=(anywhere,) * 3,
        scratch_shapes=[
            pltpu.VMEM((size, size), bf16),
            pltpu.VMEM((size, size), bf16),
            pltpu.VMEM((2, n, rows, size), bf16),
            pltpu.VMEM((2 * size, 2 * size), bf16),
            pltpu.VMEM((2 * size, 2 * size), bf16),
            pltpu.VMEM((size, size), f32),
            pltpu.VMEM((size, size), f32),
            pltpu.VMEM((size, 2 * size), f32),
            pltpu.VMEM((size, 2 * size), f32),
            pltpu.VMEM((2 * size, size), bf16),
            pltpu.VMEM((size, size), bf16),
            pltpu.VMEM((size, size), bf16),
            pltpu.VMEM((2, n, rows, size), f32),
            pltpu.VMEM((2, n, rows, size), bf16),
            pltpu.VMEM((3, n, half, size), bf16),
            pltpu.VMEM((n, half, size), bf16),
            pltpu.SemaphoreType.DMA((4,)),
            one_sem,
            one_sem,
            three,
            three,
        ]
        + [one_sem] * 8
        + [three, three]
        + [one_sem] * 4,
        compiler_params=pltpu.CompilerParams(
            collective_id=0, has_side_effects=True, vmem_limit_bytes=44 * 1024 * 1024
        ),
        cost_estimate=pl.CostEstimate(
            flops=24 * size**3 * 2, bytes_accessed=12 * size * size * 2, transcendentals=0
        ),
    )(signal, cotangent, filter_spec, *tables)


def solution(mesh):
    placed = (P(None, "dp", "seq", None), P(None, "dp", "seq", None), P(None, None, "seq", None))

    def step(signal, cotangent, filter_spec):
        if whole_sequences_fit(mesh, signal, filter_spec):
            return whole_body(mesh.shape["seq"], signal, cotangent, filter_spec)
        return body(signal, cotangent, filter_spec)

    return jax.shard_map(
        step,
        mesh=mesh,
        in_specs=placed,
        out_specs=placed,
        check_vma=False,
    )
```

```python
import functools
import math

import jax
import jax.numpy as jnp
import numpy as np
from jax import lax
from jax.experimental import pallas as pl
from jax.experimental.pallas import tpu as pltpu
from jax.sharding import PartitionSpec as P

MESH = pl.DeviceIdType.MESH

NB = 512


def unit_tables(block_size):
    steps_index = jnp.arange(block_size, dtype=jnp.int32)
    product_index = steps_index[:, None] * steps_index[None, :] % block_size
    phases = product_index.astype(jnp.float32) * (2.0 * math.pi / block_size)
    factor = 1.0 / math.sqrt(block_size)
    return (
        (jnp.cos(phases) * factor).astype(jnp.bfloat16),
        (-jnp.sin(phases) * factor).astype(jnp.bfloat16),
    )


def twiddle(row_index, col_index, length_all, orient):
    phases = (row_index[:, None] * col_index[None, :]).astype(jnp.float32) * (
        orient * 2.0 * math.pi / length_all
    )
    return (jnp.cos(phases), jnp.sin(phases))


def forward_rows(signal, tables, first_row, length_all):
    big_cos, big_sin, small_cos, small_sin = tables
    real_part = jnp.einsum("ncrs,as->ncra", signal, big_cos, preferred_element_type=jnp.float32)
    imaginary = jnp.einsum("ncrs,as->ncra", signal, big_sin, preferred_element_type=jnp.float32)
    row_index = first_row + jnp.arange(signal.shape[2], dtype=jnp.int32)
    col_index = jnp.arange(signal.shape[3], dtype=jnp.int32)
    turn_cos, turn_sin = twiddle(row_index, col_index, length_all, -1.0)
    middle = jnp.stack(
        [real_part * turn_cos - imaginary * turn_sin, real_part * turn_sin + imaginary * turn_cos]
    ).astype(jnp.bfloat16)
    received = lax.all_to_all(middle, "seq", split_axis=4, concat_axis=3, tiled=True)
    real_received = received[0]
    imaginary_received = received[1]
    out_real = jnp.einsum(
        "ncra,qr->ncaq", real_received, small_cos, preferred_element_type=jnp.float32
    ) - jnp.einsum(
        "ncra,qr->ncaq", imaginary_received, small_sin, preferred_element_type=jnp.float32
    )
    out_imaginary = jnp.einsum(
        "ncra,qr->ncaq", imaginary_received, small_cos, preferred_element_type=jnp.float32
    ) + jnp.einsum("ncra,qr->ncaq", real_received, small_sin, preferred_element_type=jnp.float32)
    return jnp.stack([out_real, out_imaginary])


def inverse_rows(spectrum, tables, first_freq, length_all):
    big_cos, big_sin, small_cos, small_sin = tables
    real_part = jnp.einsum(
        "ncaq,rq->ncar", spectrum[0], small_cos, preferred_element_type=jnp.float32
    ) + jnp.einsum("ncaq,rq->ncar", spectrum[1], small_sin, preferred_element_type=jnp.float32)
    imaginary = jnp.einsum(
        "ncaq,rq->ncar", spectrum[1], small_cos, preferred_element_type=jnp.float32
    ) - jnp.einsum("ncaq,rq->ncar", spectrum[0], small_sin, preferred_element_type=jnp.float32)
    row_index = first_freq + jnp.arange(spectrum.shape[3], dtype=jnp.int32)
    col_index = jnp.arange(spectrum.shape[4], dtype=jnp.int32)
    turn_cos, turn_sin = twiddle(row_index, col_index, length_all, 1.0)
    middle = jnp.stack(
        [real_part * turn_cos - imaginary * turn_sin, real_part * turn_sin + imaginary * turn_cos]
    ).astype(jnp.bfloat16)
    received = lax.all_to_all(middle, "seq", split_axis=4, concat_axis=3, tiled=True)
    total = jnp.einsum(
        "ncar,sa->ncrs", received[0], big_cos, preferred_element_type=jnp.float32
    ) + jnp.einsum("ncar,sa->ncrs", received[1], big_sin, preferred_element_type=jnp.float32)
    return total.astype(jnp.bfloat16)


def body(signal, cotangent, filter_spec):
    rows_total = signal.shape[2] * lax.axis_size("seq")
    big_cos, big_sin = unit_tables(NB)
    small_cos, small_sin = unit_tables(rows_total)
    tables = (big_cos, big_sin, small_cos, small_sin)
    length_all = NB * rows_total
    first_row = lax.axis_index("seq") * signal.shape[2]
    first_freq = lax.axis_index("seq") * (NB // lax.axis_size("seq"))
    filter_real = filter_spec[0].astype(jnp.float32)[:, None]
    filter_imaginary = filter_spec[1].astype(jnp.float32)[:, None]
    channels = signal.shape[1]
    stacked = forward_rows(
        jnp.concatenate([signal, cotangent], axis=1), tables, first_row, length_all
    )
    signal_spec = stacked[:, :, :channels]
    cotangent_spec = stacked[:, :, channels:]
    joined_input = jnp.concatenate(
        [
            jnp.stack(
                [
                    filter_real * signal_spec[0] - filter_imaginary * signal_spec[1],
                    filter_real * signal_spec[1] + filter_imaginary * signal_spec[0],
                ]
            ).astype(jnp.bfloat16),
            jnp.stack(
                [
                    filter_real * cotangent_spec[0] + filter_imaginary * cotangent_spec[1],
                    filter_real * cotangent_spec[1] - filter_imaginary * cotangent_spec[0],
                ]
            ).astype(jnp.bfloat16),
        ],
        axis=2,
    )
    results = inverse_rows(joined_input, tables, first_freq, length_all)
    output = results[:, :channels]
    grad_signal = results[:, channels:]
    grad_terms = jnp.stack(
        [
            jnp.sum(
                cotangent_spec[0] * signal_spec[0] + cotangent_spec[1] * signal_spec[1], axis=1
            ),
            jnp.sum(
                cotangent_spec[1] * signal_spec[0] - cotangent_spec[0] * signal_spec[1], axis=1
            ),
        ]
    )
    grad_filter = lax.psum(grad_terms, "dp")
    return (output, grad_signal, grad_filter.astype(jnp.bfloat16))


def whole_tables(size):
    index = np.arange(size)
    phases = (index[:, None] * index[None, :] % size) * (2.0 * math.pi / size)
    factor = 1.0 / math.sqrt(size)
    cos_table, sin_table = np.cos(phases) * factor, -np.sin(phases) * factor
    forward = np.block([[cos_table, sin_table], [-sin_table, cos_table]])
    turn = (index[:, None] * index[None, :]) * (2.0 * math.pi / (size * size))
    return (
        forward.astype(jnp.bfloat16),
        forward.T.astype(jnp.bfloat16),
        np.cos(turn).astype(np.float32),
        np.sin(turn).astype(np.float32),
    )


def whole_sequences_fit(mesh, signal, filter_spec):
    filters, channels, rows, size = signal.shape
    n = mesh.shape["seq"]
    return (
        mesh.shape["dp"] == 2
        and channels == 2
        and filters * channels == n
        and rows * n == size
        and filter_spec.shape[2] == rows
        and filter_spec.shape[3] == size
        and rows % 32 == 0
        and size % 256 == 0
    )


def whole_kernel(
    n,
    signal_ref,
    cotangent_ref,
    filter_ref,
    forward_ref,
    inverse_ref,
    cos_ref,
    sin_ref,
    output_ref,
    grad_signal_ref,
    grad_filter_ref,
    signal_all,
    cotangent_all,
    filter_all,
    forward_table,
    inverse_table,
    turn_cos,
    turn_sin,
    signal_spec,
    cotangent_spec,
    middle,
    output_all,
    grad_all,
    terms_wide,
    terms_mate,
    terms_out,
    terms_got,
    grad_part,
    table_sem,
    filter_send,
    filter_got,
    share_send,
    share_got,
    signal_send,
    signal_got,
    cotangent_send,
    cotangent_got,
    output_send,
    output_got,
    grad_send,
    grad_got,
    mate_send,
    mate_got,
    terms_send,
    terms_recv,
    part_send,
    part_got,
    swap_send,
    swap_got,
):
    size = signal_all.shape[0]
    rows = size // n
    half = rows // 2
    chunk = 256
    chunks = size // chunk
    per_chunk = chunk // rows
    me = lax.axis_index("seq")
    side = lax.axis_index("dp")
    other = 1 - side
    channel = lax.rem(me, 2)
    group = lax.div(me, 2)
    mate = me + 1 - 2 * channel
    my_half = pl.ds(pl.multiple_of(channel * half, half), half)
    my_rows = pl.ds(pl.multiple_of(me * rows, rows), rows)
    partners = ((side, mate), (other, me), (other, mate))

    table_copies = [
        pltpu.make_async_copy(source, target, table_sem.at[i])
        for i, (source, target) in enumerate(
            (
                (forward_ref, forward_table),
                (inverse_ref, inverse_table),
                (cos_ref, turn_cos),
                (sin_ref, turn_sin),
            )
        )
    ]
    for copy in table_copies:
        copy.start()

    barrier = pltpu.get_barrier_semaphore()

    def greet(k, carry):
        pl.semaphore_signal(
            barrier, inc=1, device_id={"dp": side, "seq": lax.rem(me + k, n)}, device_id_type=MESH
        )
        return carry

    lax.fori_loop(1, n, greet, 0)
    for to_side, to_seq in partners[1:]:
        pl.semaphore_signal(
            barrier, inc=1, device_id={"dp": to_side, "seq": to_seq}, device_id_type=MESH
        )
    pl.semaphore_wait(barrier, n + 1)

    across = n // 2
    my_part, place = lax.div(me, across), lax.rem(me, across)

    def for_peers(first, last, send):
        if first == 1:
            send((1 - my_part) * across + place)

        def one(t, carry):
            part = lax.rem(my_part + lax.rem(t + me, 2), 2)
            send(part * across + lax.rem(place + lax.div(t, 2), across))
            return carry

        lax.fori_loop(max(first, 2), last, one, 0)

    def send_all(source_of, target, send_sem, recv_sem, first=1, last=n):
        if first == 1:
            pltpu.make_async_copy(source_of(me), target, recv_sem).start()

        def send(to):
            pltpu.make_async_remote_copy(
                src_ref=source_of(to),
                dst_ref=target,
                send_sem=send_sem,
                recv_sem=recv_sem,
                device_id={"dp": side, "seq": to},
                device_id_type=MESH,
            ).start()

        for_peers(first, last, send)

    def wait_bytes(ref, sem):
        pltpu.make_async_copy(ref, ref, sem).wait()

    def filter_source(to):
        start = pl.multiple_of(lax.rem(to, 2) * half, half)
        return filter_ref.at[side, lax.div(to, 2), pl.ds(start, half), :]

    pltpu.make_async_copy(
        filter_source(me), filter_all.at[side, me, my_half, :], filter_got
    ).start()

    def send_filter(to):
        start = pl.multiple_of(lax.rem(to, 2) * half, half)
        pltpu.make_async_remote_copy(
            src_ref=filter_source(to),
            dst_ref=filter_all.at[side, me, pl.ds(start, half), :],
            send_sem=filter_send,
            recv_sem=filter_got,
            device_id={"dp": side, "seq": to},
            device_id_type=MESH,
        ).start()

    for_peers(1, n, send_filter)
    send_all(
        lambda to: signal_ref.at[lax.div(to, 2), lax.rem(to, 2)],
        signal_all.at[my_rows, :],
        signal_send,
        signal_got,
    )
    send_all(
        lambda to: cotangent_ref.at[lax.div(to, 2), lax.rem(to, 2)],
        cotangent_all.at[my_rows, :],
        cotangent_send,
        cotangent_got,
    )

    my_quarter = filter_all.at[side, :, my_half, :]
    wait_bytes(my_quarter, filter_got)
    share_copies = [
        pltpu.make_async_remote_copy(
            src_ref=my_quarter,
            dst_ref=my_quarter,
            send_sem=share_send.at[i],
            recv_sem=share_got.at[i],
            device_id={"dp": to_side, "seq": to_seq},
            device_id_type=MESH,
        )
        for i, (to_side, to_seq) in enumerate(partners)
    ]
    for copy in share_copies:
        copy.start()

    for copy in table_copies:
        copy.wait()

    def transform(values, spec, i):
        at = pl.ds(pl.multiple_of(i * chunk, chunk), chunk)
        one_signal = values[...]
        contract_last = (((1,), (1,)), ((), ()))
        real = lax.dot_general(
            forward_table[at, :size], one_signal, contract_last, preferred_element_type=jnp.float32
        )
        imaginary = lax.dot_general(
            forward_table[at, size:], one_signal, contract_last, preferred_element_type=jnp.float32
        )
        cos_part, sin_part = turn_cos[at, :], turn_sin[at, :]
        mid = jnp.concatenate(
            [
                (real * cos_part + imaginary * sin_part).astype(jnp.bfloat16),
                (imaginary * cos_part - real * sin_part).astype(jnp.bfloat16),
            ],
            axis=1,
        )
        spec[at, :] = jnp.dot(mid, forward_table[...], preferred_element_type=jnp.float32)

    def filtered(spec, sign, i):
        at = pl.ds(pl.multiple_of(i * chunk, chunk), chunk)
        blocks = pl.ds(i * per_chunk, per_chunk)
        filter_real = filter_all[0, blocks].reshape(chunk, size).astype(jnp.float32)
        filter_imaginary = filter_all[1, blocks].reshape(chunk, size).astype(jnp.float32) * sign
        real, imaginary = spec[at, :size], spec[at, size:]
        product = jnp.concatenate(
            [
                (filter_real * real - filter_imaginary * imaginary).astype(jnp.bfloat16),
                (filter_real * imaginary + filter_imaginary * real).astype(jnp.bfloat16),
            ],
            axis=1,
        )
        both = jnp.dot(product, inverse_table[...], preferred_element_type=jnp.float32)
        real, imaginary = both[:, :size], both[:, size:]
        cos_part, sin_part = turn_cos[at, :], turn_sin[at, :]
        middle[at, :] = (real * cos_part - imaginary * sin_part).astype(jnp.bfloat16)
        below = pl.ds(pl.multiple_of(size + i * chunk, chunk), chunk)
        middle[below, :] = (real * sin_part + imaginary * cos_part).astype(jnp.bfloat16)

    def restored(result, i):
        at = pl.ds(pl.multiple_of(i * chunk, chunk), chunk)
        turned = jnp.dot(
            forward_table[at, :], middle[...], preferred_element_type=jnp.float32
        )
        result[:, at] = turned.T.astype(jnp.bfloat16)

    def loop(fn):
        def one(i, carry):
            fn(i)
            return carry

        lax.fori_loop(0, chunks, one, 0)

    def rows_of(ref, to):
        return ref.at[pl.ds(pl.multiple_of(to * rows, rows), rows), :]

    wait_bytes(signal_all, signal_got)
    loop(lambda i: transform(signal_all, signal_spec, i))
    for copy in share_copies:
        copy.wait()
    loop(lambda i: filtered(signal_spec, 1.0, i))
    loop(lambda i: restored(output_all, i))
    send_all(
        lambda to: rows_of(output_all, to), output_ref.at[group, channel], output_send, output_got
    )

    wait_bytes(cotangent_all, cotangent_got)

    def transform_and_terms(i):
        transform(cotangent_all, cotangent_spec, i)
        at = pl.ds(pl.multiple_of(i * chunk, chunk), chunk)
        blocks = pl.ds(i * per_chunk, per_chunk)
        real, imaginary = signal_spec[at, :size], signal_spec[at, size:]
        back_real, back_imaginary = cotangent_spec[at, :size], cotangent_spec[at, size:]
        for part, values in enumerate(
            (
                back_real * real + back_imaginary * imaginary,
                back_imaginary * real - back_real * imaginary,
            )
        ):
            terms_wide[part, blocks] = values.reshape(per_chunk, rows, size)

    loop(transform_and_terms)
    mate_half = pl.ds(pl.multiple_of(half - channel * half, half), half)
    mate_copy = pltpu.make_async_remote_copy(
        src_ref=terms_wide.at[:, :, mate_half, :],
        dst_ref=terms_mate,
        send_sem=mate_send,
        recv_sem=mate_got,
        device_id={"dp": side, "seq": mate},
        device_id_type=MESH,
    )
    mate_copy.start()

    loop(lambda i: filtered(cotangent_spec, -1.0, i))
    mate_copy.wait()
    terms_out[...] = (terms_wide[other, :, my_half, :] + terms_mate[other]).astype(jnp.bfloat16)
    terms_copy = pltpu.make_async_remote_copy(
        src_ref=terms_out,
        dst_ref=terms_got,
        send_sem=terms_send,
        recv_sem=terms_recv,
        device_id={"dp": other, "seq": me},
        device_id_type=MESH,
    )
    terms_copy.start()
    loop(lambda i: restored(grad_all, i))
    send_grad = functools.partial(
        send_all,
        lambda to: rows_of(grad_all, to),
        grad_signal_ref.at[group, channel],
        grad_send,
        grad_got,
    )
    send_grad(1, across)

    terms_copy.wait()
    grad_part[...] = (
        terms_wide[side, :, my_half, :] + terms_mate[side] + terms_got[...].astype(jnp.float32)
    ).astype(jnp.bfloat16)
    send_all(
        lambda to: grad_part.at[to],
        grad_filter_ref.at[side, group, my_half, :],
        part_send,
        part_got,
    )
    send_grad(across, n)
    wait_bytes(grad_filter_ref.at[side], part_got)
    swap = pltpu.make_async_remote_copy(
        src_ref=grad_filter_ref.at[side],
        dst_ref=grad_filter_ref.at[side],
        send_sem=swap_send,
        recv_sem=swap_got,
        device_id={"dp": other, "seq": me},
        device_id_type=MESH,
    )
    swap.start()

    wait_bytes(output_ref, output_got)
    wait_bytes(grad_signal_ref, grad_got)
    swap.wait()
    sent = pl.ds(0, size - rows)
    wait_bytes(signal_all.at[sent, :], signal_send)
    wait_bytes(cotangent_all.at[sent, :], cotangent_send)
    wait_bytes(output_all.at[sent, :], output_send)
    wait_bytes(grad_all.at[sent, :], grad_send)
    wait_bytes(grad_part.at[pl.ds(0, n - 1)], filter_send)
    wait_bytes(grad_part.at[pl.ds(0, n - 1)], part_send)


def whole_body(n, signal, cotangent, filter_spec):
    size = signal.shape[3]
    rows = signal.shape[2]
    half = rows // 2
    tables = [jnp.asarray(table) for table in whole_tables(size)]
    bf16, f32 = jnp.bfloat16, jnp.float32
    anywhere = pl.BlockSpec(memory_space=pl.ANY)
    one_sem = pltpu.SemaphoreType.DMA(())
    three = pltpu.SemaphoreType.DMA((3,))
    return pl.pallas_call(
        functools.partial(whole_kernel, n),
        out_shape=tuple(
            jax.ShapeDtypeStruct(x.shape, x.dtype) for x in (signal, cotangent, filter_spec)
        ),
        in_specs=[pl.BlockSpec(memory_space=pltpu.HBM)] * 7,
        out_specs=(anywhere,) * 3,
        scratch_shapes=[
            pltpu.VMEM((size, size), bf16),
            pltpu.VMEM((size, size), bf16),
            pltpu.VMEM((2, n, rows, size), bf16),
            pltpu.VMEM((2 * size, 2 * size), bf16),
            pltpu.VMEM((2 * size, 2 * size), bf16),
            pltpu.VMEM((size, size), f32),
            pltpu.VMEM((size, size), f32),
            pltpu.VMEM((size, 2 * size), f32),
            pltpu.VMEM((size, 2 * size), f32),
            pltpu.VMEM((2 * size, size), bf16),
            pltpu.VMEM((size, size), bf16),
            pltpu.VMEM((size, size), bf16),
            pltpu.VMEM((2, n, rows, size), f32),
            pltpu.VMEM((2, n, half, size), f32),
            pltpu.VMEM((n, half, size), bf16),
            pltpu.VMEM((n, half, size), bf16),
            pltpu.VMEM((n, half, size), bf16),
            pltpu.SemaphoreType.DMA((4,)),
            one_sem,
            one_sem,
            three,
            three,
        ]
        + [one_sem] * 16,
        compiler_params=pltpu.CompilerParams(
            collective_id=0, has_side_effects=True, vmem_limit_bytes=60 * 1024 * 1024
        ),
        cost_estimate=pl.CostEstimate(
            flops=24 * size**3 * 2, bytes_accessed=12 * size * size * 2, transcendentals=0
        ),
    )(signal, cotangent, filter_spec, *tables)


def solution(mesh):
    placed = (P(None, "dp", "seq", None), P(None, "dp", "seq", None), P(None, None, "seq", None))

    def step(signal, cotangent, filter_spec):
        if whole_sequences_fit(mesh, signal, filter_spec):
            return whole_body(mesh.shape["seq"], signal, cotangent, filter_spec)
        return body(signal, cotangent, filter_spec)

    return jax.shard_map(
        step,
        mesh=mesh,
        in_specs=placed,
        out_specs=placed,
        check_vma=False,
    )
```

```python
import functools
import math

import jax
import jax.numpy as jnp
import numpy as np
from jax import lax
from jax.experimental import pallas as pl
from jax.experimental.pallas import tpu as pltpu
from jax.sharding import PartitionSpec as P

MESH = pl.DeviceIdType.MESH

NB = 512


def unit_tables(block_size):
    steps_index = jnp.arange(block_size, dtype=jnp.int32)
    product_index = steps_index[:, None] * steps_index[None, :] % block_size
    phases = product_index.astype(jnp.float32) * (2.0 * math.pi / block_size)
    factor = 1.0 / math.sqrt(block_size)
    return (
        (jnp.cos(phases) * factor).astype(jnp.bfloat16),
        (-jnp.sin(phases) * factor).astype(jnp.bfloat16),
    )


def twiddle(row_index, col_index, length_all, orient):
    phases = (row_index[:, None] * col_index[None, :]).astype(jnp.float32) * (
        orient * 2.0 * math.pi / length_all
    )
    return (jnp.cos(phases), jnp.sin(phases))


def forward_rows(signal, tables, first_row, length_all):
    big_cos, big_sin, small_cos, small_sin = tables
    real_part = jnp.einsum("ncrs,as->ncra", signal, big_cos, preferred_element_type=jnp.float32)
    imaginary = jnp.einsum("ncrs,as->ncra", signal, big_sin, preferred_element_type=jnp.float32)
    row_index = first_row + jnp.arange(signal.shape[2], dtype=jnp.int32)
    col_index = jnp.arange(signal.shape[3], dtype=jnp.int32)
    turn_cos, turn_sin = twiddle(row_index, col_index, length_all, -1.0)
    middle = jnp.stack(
        [real_part * turn_cos - imaginary * turn_sin, real_part * turn_sin + imaginary * turn_cos]
    ).astype(jnp.bfloat16)
    received = lax.all_to_all(middle, "seq", split_axis=4, concat_axis=3, tiled=True)
    real_received = received[0]
    imaginary_received = received[1]
    out_real = jnp.einsum(
        "ncra,qr->ncaq", real_received, small_cos, preferred_element_type=jnp.float32
    ) - jnp.einsum(
        "ncra,qr->ncaq", imaginary_received, small_sin, preferred_element_type=jnp.float32
    )
    out_imaginary = jnp.einsum(
        "ncra,qr->ncaq", imaginary_received, small_cos, preferred_element_type=jnp.float32
    ) + jnp.einsum("ncra,qr->ncaq", real_received, small_sin, preferred_element_type=jnp.float32)
    return jnp.stack([out_real, out_imaginary])


def inverse_rows(spectrum, tables, first_freq, length_all):
    big_cos, big_sin, small_cos, small_sin = tables
    real_part = jnp.einsum(
        "ncaq,rq->ncar", spectrum[0], small_cos, preferred_element_type=jnp.float32
    ) + jnp.einsum("ncaq,rq->ncar", spectrum[1], small_sin, preferred_element_type=jnp.float32)
    imaginary = jnp.einsum(
        "ncaq,rq->ncar", spectrum[1], small_cos, preferred_element_type=jnp.float32
    ) - jnp.einsum("ncaq,rq->ncar", spectrum[0], small_sin, preferred_element_type=jnp.float32)
    row_index = first_freq + jnp.arange(spectrum.shape[3], dtype=jnp.int32)
    col_index = jnp.arange(spectrum.shape[4], dtype=jnp.int32)
    turn_cos, turn_sin = twiddle(row_index, col_index, length_all, 1.0)
    middle = jnp.stack(
        [real_part * turn_cos - imaginary * turn_sin, real_part * turn_sin + imaginary * turn_cos]
    ).astype(jnp.bfloat16)
    received = lax.all_to_all(middle, "seq", split_axis=4, concat_axis=3, tiled=True)
    total = jnp.einsum(
        "ncar,sa->ncrs", received[0], big_cos, preferred_element_type=jnp.float32
    ) + jnp.einsum("ncar,sa->ncrs", received[1], big_sin, preferred_element_type=jnp.float32)
    return total.astype(jnp.bfloat16)


def body(signal, cotangent, filter_spec):
    rows_total = signal.shape[2] * lax.axis_size("seq")
    big_cos, big_sin = unit_tables(NB)
    small_cos, small_sin = unit_tables(rows_total)
    tables = (big_cos, big_sin, small_cos, small_sin)
    length_all = NB * rows_total
    first_row = lax.axis_index("seq") * signal.shape[2]
    first_freq = lax.axis_index("seq") * (NB // lax.axis_size("seq"))
    filter_real = filter_spec[0].astype(jnp.float32)[:, None]
    filter_imaginary = filter_spec[1].astype(jnp.float32)[:, None]
    channels = signal.shape[1]
    stacked = forward_rows(
        jnp.concatenate([signal, cotangent], axis=1), tables, first_row, length_all
    )
    signal_spec = stacked[:, :, :channels]
    cotangent_spec = stacked[:, :, channels:]
    joined_input = jnp.concatenate(
        [
            jnp.stack(
                [
                    filter_real * signal_spec[0] - filter_imaginary * signal_spec[1],
                    filter_real * signal_spec[1] + filter_imaginary * signal_spec[0],
                ]
            ).astype(jnp.bfloat16),
            jnp.stack(
                [
                    filter_real * cotangent_spec[0] + filter_imaginary * cotangent_spec[1],
                    filter_real * cotangent_spec[1] - filter_imaginary * cotangent_spec[0],
                ]
            ).astype(jnp.bfloat16),
        ],
        axis=2,
    )
    results = inverse_rows(joined_input, tables, first_freq, length_all)
    output = results[:, :channels]
    grad_signal = results[:, channels:]
    grad_terms = jnp.stack(
        [
            jnp.sum(
                cotangent_spec[0] * signal_spec[0] + cotangent_spec[1] * signal_spec[1], axis=1
            ),
            jnp.sum(
                cotangent_spec[1] * signal_spec[0] - cotangent_spec[0] * signal_spec[1], axis=1
            ),
        ]
    )
    grad_filter = lax.psum(grad_terms, "dp")
    return (output, grad_signal, grad_filter.astype(jnp.bfloat16))


def whole_tables(size):
    index = np.arange(size)
    phases = (index[:, None] * index[None, :] % size) * (2.0 * math.pi / size)
    factor = 1.0 / math.sqrt(size)
    cos_table, sin_table = np.cos(phases) * factor, -np.sin(phases) * factor
    forward = np.block([[cos_table, sin_table], [-sin_table, cos_table]])
    turn = (index[:, None] * index[None, :]) * (2.0 * math.pi / (size * size))
    return (
        forward.astype(jnp.bfloat16),
        forward.T.astype(jnp.bfloat16),
        np.cos(turn).astype(np.float32),
        np.sin(turn).astype(np.float32),
    )


def whole_sequences_fit(mesh, signal, filter_spec):
    filters, channels, rows, size = signal.shape
    n = mesh.shape["seq"]
    return (
        mesh.shape["dp"] == 2
        and channels == 2
        and filters * channels == n
        and rows * n == size
        and filter_spec.shape[2] == rows
        and filter_spec.shape[3] == size
        and rows % 32 == 0
        and size % 256 == 0
    )


def whole_kernel(
    n,
    signal_ref,
    cotangent_ref,
    filter_ref,
    forward_ref,
    inverse_ref,
    cos_ref,
    sin_ref,
    output_ref,
    grad_signal_ref,
    grad_filter_ref,
    signal_all,
    cotangent_all,
    filter_all,
    forward_table,
    inverse_table,
    turn_cos,
    turn_sin,
    signal_spec,
    cotangent_spec,
    middle,
    output_all,
    grad_all,
    terms_wide,
    terms_mate,
    terms_out,
    terms_got,
    grad_part,
    table_sem,
    filter_send,
    filter_got,
    share_send,
    share_got,
    signal_send,
    signal_got,
    cotangent_send,
    cotangent_got,
    output_send,
    output_got,
    grad_send,
    grad_got,
    mate_send,
    mate_got,
    terms_send,
    terms_recv,
    part_send,
    part_got,
    swap_send,
    swap_got,
):
    size = signal_all.shape[0]
    rows = size // n
    half = rows // 2
    chunk = 256
    chunks = size // chunk
    per_chunk = chunk // rows
    me = lax.axis_index("seq")
    side = lax.axis_index("dp")
    other = 1 - side
    channel = lax.rem(me, 2)
    group = lax.div(me, 2)
    mate = me + 1 - 2 * channel
    my_half = pl.ds(pl.multiple_of(channel * half, half), half)
    my_rows = pl.ds(pl.multiple_of(me * rows, rows), rows)
    partners = ((side, mate), (other, me), (other, mate))

    table_copies = [
        pltpu.make_async_copy(source, target, table_sem.at[i])
        for i, (source, target) in enumerate(
            (
                (forward_ref, forward_table),
                (inverse_ref, inverse_table),
                (cos_ref, turn_cos),
                (sin_ref, turn_sin),
            )
        )
    ]
    for copy in table_copies:
        copy.start()

    barrier = pltpu.get_barrier_semaphore()

    def greet(k, carry):
        pl.semaphore_signal(
            barrier, inc=1, device_id={"dp": side, "seq": lax.rem(me + k, n)}, device_id_type=MESH
        )
        return carry

    lax.fori_loop(1, n, greet, 0)
    for to_side, to_seq in partners[1:]:
        pl.semaphore_signal(
            barrier, inc=1, device_id={"dp": to_side, "seq": to_seq}, device_id_type=MESH
        )
    pl.semaphore_wait(barrier, n + 1)

    across = n // 2
    my_part, place = lax.div(me, across), lax.rem(me, across)

    def for_peers(first, last, send):
        if first == 1:
            send((1 - my_part) * across + place)

        def one(t, carry):
            part = lax.rem(my_part + lax.rem(t + me, 2), 2)
            send(part * across + lax.rem(place + lax.div(t, 2), across))
            return carry

        lax.fori_loop(max(first, 2), last, one, 0)

    def send_all(source_of, target, send_sem, recv_sem, first=1, last=n):
        if first == 1:
            pltpu.make_async_copy(source_of(me), target, recv_sem).start()

        def send(to):
            pltpu.make_async_remote_copy(
                src_ref=source_of(to),
                dst_ref=target,
                send_sem=send_sem,
                recv_sem=recv_sem,
                device_id={"dp": side, "seq": to},
                device_id_type=MESH,
            ).start()

        for_peers(first, last, send)

    def wait_bytes(ref, sem):
        pltpu.make_async_copy(ref, ref, sem).wait()

    def filter_source(to):
        start = pl.multiple_of(lax.rem(to, 2) * half, half)
        return filter_ref.at[side, lax.div(to, 2), pl.ds(start, half), :]

    pltpu.make_async_copy(
        filter_source(me), filter_all.at[side, me, my_half, :], filter_got
    ).start()

    def send_filter(to):
        start = pl.multiple_of(lax.rem(to, 2) * half, half)
        pltpu.make_async_remote_copy(
            src_ref=filter_source(to),
            dst_ref=filter_all.at[side, me, pl.ds(start, half), :],
            send_sem=filter_send,
            recv_sem=filter_got,
            device_id={"dp": side, "seq": to},
            device_id_type=MESH,
        ).start()

    for_peers(1, n, send_filter)
    send_all(
        lambda to: signal_ref.at[lax.div(to, 2), lax.rem(to, 2)],
        signal_all.at[my_rows, :],
        signal_send,
        signal_got,
    )

    my_quarter = filter_all.at[side, :, my_half, :]
    wait_bytes(my_quarter, filter_got)
    other_quarter = filter_all.at[other, :, my_half, :]
    share_copies = [
        pltpu.make_async_remote_copy(
            src_ref=quarter,
            dst_ref=quarter,
            send_sem=share_send.at[i],
            recv_sem=share_got.at[i],
            device_id={"dp": to_side, "seq": to_seq},
            device_id_type=MESH,
        )
        for i, (quarter, to_side, to_seq) in enumerate(
            (
                (my_quarter, other, me),
                (my_quarter, side, mate),
                (other_quarter, side, mate),
            )
        )
    ]
    share_copies[0].start()
    share_copies[1].start()
    send_all(
        lambda to: cotangent_ref.at[lax.div(to, 2), lax.rem(to, 2)],
        cotangent_all.at[my_rows, :],
        cotangent_send,
        cotangent_got,
    )
    share_copies[0].wait_recv()
    share_copies[2].start()

    for copy in table_copies:
        copy.wait()

    def transform(values, spec, i):
        at = pl.ds(pl.multiple_of(i * chunk, chunk), chunk)
        one_signal = values[...]
        contract_last = (((1,), (1,)), ((), ()))
        real = lax.dot_general(
            forward_table[at, :size], one_signal, contract_last, preferred_element_type=jnp.float32
        )
        imaginary = lax.dot_general(
            forward_table[at, size:], one_signal, contract_last, preferred_element_type=jnp.float32
        )
        cos_part, sin_part = turn_cos[at, :], turn_sin[at, :]
        mid = jnp.concatenate(
            [
                (real * cos_part + imaginary * sin_part).astype(jnp.bfloat16),
                (imaginary * cos_part - real * sin_part).astype(jnp.bfloat16),
            ],
            axis=1,
        )
        spec[at, :] = jnp.dot(mid, forward_table[...], preferred_element_type=jnp.float32)

    def filtered(spec, sign, i):
        at = pl.ds(pl.multiple_of(i * chunk, chunk), chunk)
        blocks = pl.ds(i * per_chunk, per_chunk)
        filter_real = filter_all[0, blocks].reshape(chunk, size).astype(jnp.float32)
        filter_imaginary = filter_all[1, blocks].reshape(chunk, size).astype(jnp.float32) * sign
        real, imaginary = spec[at, :size], spec[at, size:]
        product = jnp.concatenate(
            [
                (filter_real * real - filter_imaginary * imaginary).astype(jnp.bfloat16),
                (filter_real * imaginary + filter_imaginary * real).astype(jnp.bfloat16),
            ],
            axis=1,
        )
        both = jnp.dot(product, inverse_table[...], preferred_element_type=jnp.float32)
        real, imaginary = both[:, :size], both[:, size:]
        cos_part, sin_part = turn_cos[at, :], turn_sin[at, :]
        middle[at, :] = (real * cos_part - imaginary * sin_part).astype(jnp.bfloat16)
        below = pl.ds(pl.multiple_of(size + i * chunk, chunk), chunk)
        middle[below, :] = (real * sin_part + imaginary * cos_part).astype(jnp.bfloat16)

    def restored(result, i):
        at = pl.ds(pl.multiple_of(i * chunk, chunk), chunk)
        turned = jnp.dot(
            forward_table[at, :], middle[...], preferred_element_type=jnp.float32
        )
        result[:, at] = turned.T.astype(jnp.bfloat16)

    def loop(fn):
        def one(i, carry):
            fn(i)
            return carry

        lax.fori_loop(0, chunks, one, 0)

    def rows_of(ref, to):
        return ref.at[pl.ds(pl.multiple_of(to * rows, rows), rows), :]

    wait_bytes(signal_all, signal_got)
    loop(lambda i: transform(signal_all, signal_spec, i))
    share_copies[0].wait_send()
    share_copies[1].wait()
    share_copies[2].wait()
    loop(lambda i: filtered(signal_spec, 1.0, i))
    loop(lambda i: restored(output_all, i))
    send_all(
        lambda to: rows_of(output_all, to), output_ref.at[group, channel], output_send, output_got
    )

    wait_bytes(cotangent_all, cotangent_got)

    def transform_and_terms(i):
        transform(cotangent_all, cotangent_spec, i)
        at = pl.ds(pl.multiple_of(i * chunk, chunk), chunk)
        blocks = pl.ds(i * per_chunk, per_chunk)
        real, imaginary = signal_spec[at, :size], signal_spec[at, size:]
        back_real, back_imaginary = cotangent_spec[at, :size], cotangent_spec[at, size:]
        for part, values in enumerate(
            (
                back_real * real + back_imaginary * imaginary,
                back_imaginary * real - back_real * imaginary,
            )
        ):
            terms_wide[part, blocks] = values.reshape(per_chunk, rows, size)

    loop(transform_and_terms)
    mate_half = pl.ds(pl.multiple_of(half - channel * half, half), half)
    mate_copy = pltpu.make_async_remote_copy(
        src_ref=terms_wide.at[:, :, mate_half, :],
        dst_ref=terms_mate,
        send_sem=mate_send,
        recv_sem=mate_got,
        device_id={"dp": side, "seq": mate},
        device_id_type=MESH,
    )
    mate_copy.start()

    loop(lambda i: filtered(cotangent_spec, -1.0, i))
    mate_copy.wait()
    terms_out[...] = (terms_wide[other, :, my_half, :] + terms_mate[other]).astype(jnp.bfloat16)
    terms_copy = pltpu.make_async_remote_copy(
        src_ref=terms_out,
        dst_ref=terms_got,
        send_sem=terms_send,
        recv_sem=terms_recv,
        device_id={"dp": other, "seq": me},
        device_id_type=MESH,
    )
    terms_copy.start()
    loop(lambda i: restored(grad_all, i))
    send_grad = functools.partial(
        send_all,
        lambda to: rows_of(grad_all, to),
        grad_signal_ref.at[group, channel],
        grad_send,
        grad_got,
    )
    send_grad(1, across)

    terms_copy.wait()
    grad_part[...] = (
        terms_wide[side, :, my_half, :] + terms_mate[side] + terms_got[...].astype(jnp.float32)
    ).astype(jnp.bfloat16)
    send_all(
        lambda to: grad_part.at[to],
        grad_filter_ref.at[side, group, my_half, :],
        part_send,
        part_got,
    )
    send_grad(across, n)
    wait_bytes(grad_filter_ref.at[side], part_got)
    swap = pltpu.make_async_remote_copy(
        src_ref=grad_filter_ref.at[side],
        dst_ref=grad_filter_ref.at[side],
        send_sem=swap_send,
        recv_sem=swap_got,
        device_id={"dp": other, "seq": me},
        device_id_type=MESH,
    )
    swap.start()

    wait_bytes(output_ref, output_got)
    wait_bytes(grad_signal_ref, grad_got)
    swap.wait()
    sent = pl.ds(0, size - rows)
    wait_bytes(signal_all.at[sent, :], signal_send)
    wait_bytes(cotangent_all.at[sent, :], cotangent_send)
    wait_bytes(output_all.at[sent, :], output_send)
    wait_bytes(grad_all.at[sent, :], grad_send)
    wait_bytes(grad_part.at[pl.ds(0, n - 1)], filter_send)
    wait_bytes(grad_part.at[pl.ds(0, n - 1)], part_send)


DEPTH = 2


def hand_over_kernel(a_in, b_in, c_in, a_out, b_out, c_out, a_held, b_held, c_held, read, wrote):
    reads, writes = [], []
    for source, target, held in (
        (a_in, a_out, a_held),
        (b_in, b_out, b_held),
        (c_in, c_out, c_held),
    ):
        part = source.shape[0] // DEPTH
        for i in range(DEPTH):
            at, sem = pl.ds(i * part, part), len(reads)
            reads.append(pltpu.make_async_copy(source.at[at], held.at[at], read.at[sem]))
            writes.append(pltpu.make_async_copy(held.at[at], target.at[at], wrote.at[sem]))
    for copy in reads:
        copy.start()
    for before, after in zip(reads, writes):
        before.wait()
        after.start()
    for copy in writes:
        copy.wait()


def whole_body(n, signal, cotangent, filter_spec):
    size = signal.shape[3]
    rows = signal.shape[2]
    half = rows // 2
    tables = [jnp.asarray(table) for table in whole_tables(size)]
    bf16, f32 = jnp.bfloat16, jnp.float32
    anywhere = pl.BlockSpec(memory_space=pl.ANY)
    one_sem = pltpu.SemaphoreType.DMA(())
    three = pltpu.SemaphoreType.DMA((3,))
    landed = pl.pallas_call(
        functools.partial(whole_kernel, n),
        out_shape=tuple(
            jax.ShapeDtypeStruct(x.shape, x.dtype) for x in (signal, cotangent, filter_spec)
        ),
        in_specs=[pl.BlockSpec(memory_space=pltpu.HBM)] * 7,
        out_specs=(anywhere,) * 3,
        scratch_shapes=[
            pltpu.VMEM((size, size), bf16),
            pltpu.VMEM((size, size), bf16),
            pltpu.VMEM((2, n, rows, size), bf16),
            pltpu.VMEM((2 * size, 2 * size), bf16),
            pltpu.VMEM((2 * size, 2 * size), bf16),
            pltpu.VMEM((size, size), f32),
            pltpu.VMEM((size, size), f32),
            pltpu.VMEM((size, 2 * size), f32),
            pltpu.VMEM((size, 2 * size), f32),
            pltpu.VMEM((2 * size, size), bf16),
            pltpu.VMEM((size, size), bf16),
            pltpu.VMEM((size, size), bf16),
            pltpu.VMEM((2, n, rows, size), f32),
            pltpu.VMEM((2, n, half, size), f32),
            pltpu.VMEM((n, half, size), bf16),
            pltpu.VMEM((n, half, size), bf16),
            pltpu.VMEM((n, half, size), bf16),
            pltpu.SemaphoreType.DMA((4,)),
            one_sem,
            one_sem,
            three,
            three,
        ]
        + [one_sem] * 16,
        compiler_params=pltpu.CompilerParams(
            collective_id=0, has_side_effects=True, vmem_limit_bytes=60 * 1024 * 1024
        ),
        cost_estimate=pl.CostEstimate(
            flops=24 * size**3 * 2, bytes_accessed=12 * size * size * 2, transcendentals=0
        ),
    )(signal, cotangent, filter_spec, *tables)
    pieces = 3 * DEPTH
    return pl.pallas_call(
        hand_over_kernel,
        out_shape=tuple(jax.ShapeDtypeStruct(x.shape, x.dtype) for x in landed),
        in_specs=[anywhere] * 3,
        out_specs=(anywhere,) * 3,
        scratch_shapes=[pltpu.VMEM(x.shape, x.dtype) for x in landed]
        + [pltpu.SemaphoreType.DMA((pieces,))] * 2,
        compiler_params=pltpu.CompilerParams(vmem_limit_bytes=60 * 1024 * 1024),
        cost_estimate=pl.CostEstimate(
            flops=0, bytes_accessed=12 * rows * n * size, transcendentals=0
        ),
    )(*landed)


def solution(mesh):
    placed = (P(None, "dp", "seq", None), P(None, "dp", "seq", None), P(None, None, "seq", None))

    def step(signal, cotangent, filter_spec):
        if whole_sequences_fit(mesh, signal, filter_spec):
            return whole_body(mesh.shape["seq"], signal, cotangent, filter_spec)
        return body(signal, cotangent, filter_spec)

    return jax.shard_map(
        step,
        mesh=mesh,
        in_specs=placed,
        out_specs=placed,
        check_vma=False,
    )
```

```python
import functools
import math

import jax
import jax.numpy as jnp
import numpy as np
from jax import lax
from jax.experimental import pallas as pl
from jax.experimental.pallas import tpu as pltpu
from jax.sharding import PartitionSpec as P

MESH = pl.DeviceIdType.MESH

NB = 512


def unit_tables(block_size):
    steps_index = jnp.arange(block_size, dtype=jnp.int32)
    product_index = steps_index[:, None] * steps_index[None, :] % block_size
    phases = product_index.astype(jnp.float32) * (2.0 * math.pi / block_size)
    factor = 1.0 / math.sqrt(block_size)
    return (
        (jnp.cos(phases) * factor).astype(jnp.bfloat16),
        (-jnp.sin(phases) * factor).astype(jnp.bfloat16),
    )


def twiddle(row_index, col_index, length_all, orient):
    phases = (row_index[:, None] * col_index[None, :]).astype(jnp.float32) * (
        orient * 2.0 * math.pi / length_all
    )
    return (jnp.cos(phases), jnp.sin(phases))


def forward_rows(signal, tables, first_row, length_all):
    big_cos, big_sin, small_cos, small_sin = tables
    real_part = jnp.einsum("ncrs,as->ncra", signal, big_cos, preferred_element_type=jnp.float32)
    imaginary = jnp.einsum("ncrs,as->ncra", signal, big_sin, preferred_element_type=jnp.float32)
    row_index = first_row + jnp.arange(signal.shape[2], dtype=jnp.int32)
    col_index = jnp.arange(signal.shape[3], dtype=jnp.int32)
    turn_cos, turn_sin = twiddle(row_index, col_index, length_all, -1.0)
    middle = jnp.stack(
        [real_part * turn_cos - imaginary * turn_sin, real_part * turn_sin + imaginary * turn_cos]
    ).astype(jnp.bfloat16)
    received = lax.all_to_all(middle, "seq", split_axis=4, concat_axis=3, tiled=True)
    real_received = received[0]
    imaginary_received = received[1]
    out_real = jnp.einsum(
        "ncra,qr->ncaq", real_received, small_cos, preferred_element_type=jnp.float32
    ) - jnp.einsum(
        "ncra,qr->ncaq", imaginary_received, small_sin, preferred_element_type=jnp.float32
    )
    out_imaginary = jnp.einsum(
        "ncra,qr->ncaq", imaginary_received, small_cos, preferred_element_type=jnp.float32
    ) + jnp.einsum("ncra,qr->ncaq", real_received, small_sin, preferred_element_type=jnp.float32)
    return jnp.stack([out_real, out_imaginary])


def inverse_rows(spectrum, tables, first_freq, length_all):
    big_cos, big_sin, small_cos, small_sin = tables
    real_part = jnp.einsum(
        "ncaq,rq->ncar", spectrum[0], small_cos, preferred_element_type=jnp.float32
    ) + jnp.einsum("ncaq,rq->ncar", spectrum[1], small_sin, preferred_element_type=jnp.float32)
    imaginary = jnp.einsum(
        "ncaq,rq->ncar", spectrum[1], small_cos, preferred_element_type=jnp.float32
    ) - jnp.einsum("ncaq,rq->ncar", spectrum[0], small_sin, preferred_element_type=jnp.float32)
    row_index = first_freq + jnp.arange(spectrum.shape[3], dtype=jnp.int32)
    col_index = jnp.arange(spectrum.shape[4], dtype=jnp.int32)
    turn_cos, turn_sin = twiddle(row_index, col_index, length_all, 1.0)
    middle = jnp.stack(
        [real_part * turn_cos - imaginary * turn_sin, real_part * turn_sin + imaginary * turn_cos]
    ).astype(jnp.bfloat16)
    received = lax.all_to_all(middle, "seq", split_axis=4, concat_axis=3, tiled=True)
    total = jnp.einsum(
        "ncar,sa->ncrs", received[0], big_cos, preferred_element_type=jnp.float32
    ) + jnp.einsum("ncar,sa->ncrs", received[1], big_sin, preferred_element_type=jnp.float32)
    return total.astype(jnp.bfloat16)


def body(signal, cotangent, filter_spec):
    rows_total = signal.shape[2] * lax.axis_size("seq")
    big_cos, big_sin = unit_tables(NB)
    small_cos, small_sin = unit_tables(rows_total)
    tables = (big_cos, big_sin, small_cos, small_sin)
    length_all = NB * rows_total
    first_row = lax.axis_index("seq") * signal.shape[2]
    first_freq = lax.axis_index("seq") * (NB // lax.axis_size("seq"))
    filter_real = filter_spec[0].astype(jnp.float32)[:, None]
    filter_imaginary = filter_spec[1].astype(jnp.float32)[:, None]
    channels = signal.shape[1]
    stacked = forward_rows(
        jnp.concatenate([signal, cotangent], axis=1), tables, first_row, length_all
    )
    signal_spec = stacked[:, :, :channels]
    cotangent_spec = stacked[:, :, channels:]
    joined_input = jnp.concatenate(
        [
            jnp.stack(
                [
                    filter_real * signal_spec[0] - filter_imaginary * signal_spec[1],
                    filter_real * signal_spec[1] + filter_imaginary * signal_spec[0],
                ]
            ).astype(jnp.bfloat16),
            jnp.stack(
                [
                    filter_real * cotangent_spec[0] + filter_imaginary * cotangent_spec[1],
                    filter_real * cotangent_spec[1] - filter_imaginary * cotangent_spec[0],
                ]
            ).astype(jnp.bfloat16),
        ],
        axis=2,
    )
    results = inverse_rows(joined_input, tables, first_freq, length_all)
    output = results[:, :channels]
    grad_signal = results[:, channels:]
    grad_terms = jnp.stack(
        [
            jnp.sum(
                cotangent_spec[0] * signal_spec[0] + cotangent_spec[1] * signal_spec[1], axis=1
            ),
            jnp.sum(
                cotangent_spec[1] * signal_spec[0] - cotangent_spec[0] * signal_spec[1], axis=1
            ),
        ]
    )
    grad_filter = lax.psum(grad_terms, "dp")
    return (output, grad_signal, grad_filter.astype(jnp.bfloat16))


def whole_tables(size):
    index = np.arange(size)
    phases = (index[:, None] * index[None, :] % size) * (2.0 * math.pi / size)
    factor = 1.0 / math.sqrt(size)
    cos_table, sin_table = np.cos(phases) * factor, -np.sin(phases) * factor
    forward = np.block([[cos_table, sin_table], [-sin_table, cos_table]])
    turn = (index[:, None] * index[None, :]) * (2.0 * math.pi / (size * size))
    return (
        forward.astype(jnp.bfloat16),
        forward.T.astype(jnp.bfloat16),
        np.cos(turn).astype(np.float32),
        np.sin(turn).astype(np.float32),
    )


def whole_sequences_fit(mesh, signal, filter_spec):
    filters, channels, rows, size = signal.shape
    n = mesh.shape["seq"]
    return (
        mesh.shape["dp"] == 2
        and channels == 2
        and filters * channels == n
        and rows * n == size
        and filter_spec.shape[2] == rows
        and filter_spec.shape[3] == size
        and rows % 32 == 0
        and size % 256 == 0
    )


def whole_kernel(
    n,
    signal_ref,
    cotangent_ref,
    filter_ref,
    forward_ref,
    inverse_ref,
    cos_ref,
    sin_ref,
    output_ref,
    grad_signal_ref,
    grad_filter_ref,
    signal_all,
    cotangent_all,
    filter_all,
    forward_table,
    inverse_table,
    turn_cos,
    turn_sin,
    signal_spec,
    cotangent_spec,
    middle,
    output_all,
    grad_all,
    terms_wide,
    terms_mate,
    terms_out,
    terms_got,
    grad_part,
    table_sem,
    filter_send,
    filter_got,
    share_send,
    share_got,
    signal_send,
    signal_got,
    cotangent_send,
    cotangent_got,
    output_send,
    output_got,
    grad_send,
    grad_got,
    mate_send,
    mate_got,
    terms_send,
    terms_recv,
    part_send,
    part_got,
    swap_send,
    swap_got,
):
    size = signal_all.shape[0]
    rows = size // n
    half = rows // 2
    chunks = 2
    chunk = size // chunks
    per_chunk = chunk // rows
    me = lax.axis_index("seq")
    side = lax.axis_index("dp")
    other = 1 - side
    channel = lax.rem(me, 2)
    group = lax.div(me, 2)
    mate = me + 1 - 2 * channel
    my_half = pl.ds(pl.multiple_of(channel * half, half), half)
    my_rows = pl.ds(pl.multiple_of(me * rows, rows), rows)
    partners = ((side, mate), (other, me), (other, mate))

    table_copies = [
        pltpu.make_async_copy(source, target, table_sem.at[i])
        for i, (source, target) in enumerate(
            (
                (forward_ref, forward_table),
                (inverse_ref, inverse_table),
                (cos_ref, turn_cos),
                (sin_ref, turn_sin),
            )
        )
    ]
    for copy in table_copies:
        copy.start()

    barrier = pltpu.get_barrier_semaphore()

    def greet(k, carry):
        pl.semaphore_signal(
            barrier, inc=1, device_id={"dp": side, "seq": lax.rem(me + k, n)}, device_id_type=MESH
        )
        return carry

    lax.fori_loop(1, n, greet, 0)
    for to_side, to_seq in partners[1:]:
        pl.semaphore_signal(
            barrier, inc=1, device_id={"dp": to_side, "seq": to_seq}, device_id_type=MESH
        )
    pl.semaphore_wait(barrier, n + 1)

    across = n // 2
    my_part, place = lax.div(me, across), lax.rem(me, across)

    def for_peers(first, last, send):
        if first == 1:
            send((1 - my_part) * across + place)

        def one(t, carry):
            part = lax.rem(my_part + lax.rem(t + me, 2), 2)
            send(part * across + lax.rem(place + lax.div(t, 2), across))
            return carry

        lax.fori_loop(max(first, 2), last, one, 0)

    def send_all(source_of, target, send_sem, recv_sem, first=1, last=n):
        if first == 1:
            pltpu.make_async_copy(source_of(me), target, recv_sem).start()

        def send(to):
            pltpu.make_async_remote_copy(
                src_ref=source_of(to),
                dst_ref=target,
                send_sem=send_sem,
                recv_sem=recv_sem,
                device_id={"dp": side, "seq": to},
                device_id_type=MESH,
            ).start()

        for_peers(first, last, send)

    def wait_bytes(ref, sem):
        pltpu.make_async_copy(ref, ref, sem).wait()

    def filter_source(to):
        start = pl.multiple_of(lax.rem(to, 2) * half, half)
        return filter_ref.at[side, lax.div(to, 2), pl.ds(start, half), :]

    pltpu.make_async_copy(
        filter_source(me), filter_all.at[side, me, my_half, :], filter_got
    ).start()

    def send_filter(to):
        start = pl.multiple_of(lax.rem(to, 2) * half, half)
        pltpu.make_async_remote_copy(
            src_ref=filter_source(to),
            dst_ref=filter_all.at[side, me, pl.ds(start, half), :],
            send_sem=filter_send,
            recv_sem=filter_got,
            device_id={"dp": side, "seq": to},
            device_id_type=MESH,
        ).start()

    for_peers(1, n, send_filter)
    send_all(
        lambda to: signal_ref.at[lax.div(to, 2), lax.rem(to, 2)],
        signal_all.at[my_rows, :],
        signal_send,
        signal_got,
    )

    my_quarter = filter_all.at[side, :, my_half, :]
    wait_bytes(my_quarter, filter_got)
    other_quarter = filter_all.at[other, :, my_half, :]
    share_copies = [
        pltpu.make_async_remote_copy(
            src_ref=quarter,
            dst_ref=quarter,
            send_sem=share_send.at[i],
            recv_sem=share_got.at[i],
            device_id={"dp": to_side, "seq": to_seq},
            device_id_type=MESH,
        )
        for i, (quarter, to_side, to_seq) in enumerate(
            (
                (my_quarter, other, me),
                (my_quarter, side, mate),
                (other_quarter, side, mate),
            )
        )
    ]
    share_copies[0].start()
    share_copies[1].start()
    send_cotangent = functools.partial(
        send_all,
        lambda to: cotangent_ref.at[lax.div(to, 2), lax.rem(to, 2)],
        cotangent_all.at[my_rows, :],
        cotangent_send,
        cotangent_got,
    )
    early = max(2, n // 3)
    send_cotangent(1, early)
    share_copies[0].wait_recv()
    share_copies[2].start()

    for copy in table_copies:
        copy.wait()

    def transform(values, spec, i):
        at = pl.ds(pl.multiple_of(i * chunk, chunk), chunk)
        one_signal = values[...]
        contract_last = (((1,), (1,)), ((), ()))
        real = lax.dot_general(
            forward_table[at, :size], one_signal, contract_last, preferred_element_type=jnp.float32
        )
        imaginary = lax.dot_general(
            forward_table[at, size:], one_signal, contract_last, preferred_element_type=jnp.float32
        )
        cos_part, sin_part = turn_cos[at, :], turn_sin[at, :]
        mid = jnp.concatenate(
            [
                (real * cos_part + imaginary * sin_part).astype(jnp.bfloat16),
                (imaginary * cos_part - real * sin_part).astype(jnp.bfloat16),
            ],
            axis=1,
        )
        spec[at, :] = jnp.dot(mid, forward_table[...], preferred_element_type=jnp.float32)

    def filtered(spec, sign, i):
        at = pl.ds(pl.multiple_of(i * chunk, chunk), chunk)
        blocks = pl.ds(i * per_chunk, per_chunk)
        filter_real = filter_all[0, blocks].reshape(chunk, size).astype(jnp.float32)
        filter_imaginary = filter_all[1, blocks].reshape(chunk, size).astype(jnp.float32) * sign
        real, imaginary = spec[at, :size], spec[at, size:]
        product = jnp.concatenate(
            [
                (filter_real * real - filter_imaginary * imaginary).astype(jnp.bfloat16),
                (filter_real * imaginary + filter_imaginary * real).astype(jnp.bfloat16),
            ],
            axis=1,
        )
        both = jnp.dot(product, inverse_table[...], preferred_element_type=jnp.float32)
        real, imaginary = both[:, :size], both[:, size:]
        cos_part, sin_part = turn_cos[at, :], turn_sin[at, :]
        middle[at, :] = (real * cos_part - imaginary * sin_part).astype(jnp.bfloat16)
        below = pl.ds(pl.multiple_of(size + i * chunk, chunk), chunk)
        middle[below, :] = (real * sin_part + imaginary * cos_part).astype(jnp.bfloat16)

    def restored(result, i):
        at = pl.ds(pl.multiple_of(i * chunk, chunk), chunk)
        turned = jnp.dot(
            forward_table[:size, :], middle[:, at], preferred_element_type=jnp.float32
        )
        result[at, :] = turned.T.astype(jnp.bfloat16)

    def send_rows(result, target, send_sem, recv_sem, part, first, last):
        def one(k, carry):
            to = part * across + lax.rem(place + k, across)
            pltpu.make_async_remote_copy(
                src_ref=rows_of(result, to),
                dst_ref=target,
                send_sem=send_sem,
                recv_sem=recv_sem,
                device_id={"dp": side, "seq": to},
                device_id_type=MESH,
            ).start()
            return carry

        lax.fori_loop(first, last, one, 0)

    def loop(fn):
        def one(i, carry):
            fn(i)
            return carry

        lax.fori_loop(0, chunks, one, 0)

    def rows_of(ref, to):
        return ref.at[pl.ds(pl.multiple_of(to * rows, rows), rows), :]

    wait_bytes(signal_all, signal_got)
    send_cotangent(early, n)
    loop(lambda i: transform(signal_all, signal_spec, i))
    share_copies[0].wait_send()
    share_copies[1].wait()
    share_copies[2].wait()
    loop(lambda i: filtered(signal_spec, 1.0, i))
    there = 1 - my_part
    send_output = functools.partial(
        send_rows, output_all, output_ref.at[group, channel], output_send, output_got
    )
    restored(output_all, there)
    send_output(there, 0, across)
    restored(output_all, my_part)
    send_output(my_part, 1, across)
    pltpu.make_async_copy(
        rows_of(output_all, me), output_ref.at[group, channel], output_got
    ).start()

    wait_bytes(cotangent_all, cotangent_got)

    def transform_and_terms(i):
        transform(cotangent_all, cotangent_spec, i)
        at = pl.ds(pl.multiple_of(i * chunk, chunk), chunk)
        blocks = pl.ds(i * per_chunk, per_chunk)
        real, imaginary = signal_spec[at, :size], signal_spec[at, size:]
        back_real, back_imaginary = cotangent_spec[at, :size], cotangent_spec[at, size:]
        for part, values in enumerate(
            (
                back_real * real + back_imaginary * imaginary,
                back_imaginary * real - back_real * imaginary,
            )
        ):
            terms_wide[part, blocks] = values.reshape(per_chunk, rows, size)

    loop(transform_and_terms)
    mate_half = pl.ds(pl.multiple_of(half - channel * half, half), half)
    mate_copy = pltpu.make_async_remote_copy(
        src_ref=terms_wide.at[:, :, mate_half, :],
        dst_ref=terms_mate,
        send_sem=mate_send,
        recv_sem=mate_got,
        device_id={"dp": side, "seq": mate},
        device_id_type=MESH,
    )
    mate_copy.start()

    loop(lambda i: filtered(cotangent_spec, -1.0, i))
    mate_copy.wait()
    terms_out[...] = (terms_wide[other, :, my_half, :] + terms_mate[other]).astype(jnp.bfloat16)
    terms_copy = pltpu.make_async_remote_copy(
        src_ref=terms_out,
        dst_ref=terms_got,
        send_sem=terms_send,
        recv_sem=terms_recv,
        device_id={"dp": other, "seq": me},
        device_id_type=MESH,
    )
    terms_copy.start()
    send_grad = functools.partial(
        send_rows, grad_all, grad_signal_ref.at[group, channel], grad_send, grad_got
    )
    restored(grad_all, there)
    send_grad(there, 0, across // 2)
    restored(grad_all, my_part)
    pltpu.make_async_copy(
        rows_of(grad_all, me), grad_signal_ref.at[group, channel], grad_got
    ).start()

    terms_copy.wait()
    grad_part[...] = (
        terms_wide[side, :, my_half, :] + terms_mate[side] + terms_got[...].astype(jnp.float32)
    ).astype(jnp.bfloat16)
    send_all(
        lambda to: grad_part.at[to],
        grad_filter_ref.at[side, group, my_half, :],
        part_send,
        part_got,
    )
    send_grad(there, across // 2, across)
    send_grad(my_part, 1, across)
    wait_bytes(grad_filter_ref.at[side], part_got)
    swap = pltpu.make_async_remote_copy(
        src_ref=grad_filter_ref.at[side],
        dst_ref=grad_filter_ref.at[side],
        send_sem=swap_send,
        recv_sem=swap_got,
        device_id={"dp": other, "seq": me},
        device_id_type=MESH,
    )
    swap.start()

    wait_bytes(output_ref, output_got)
    wait_bytes(grad_signal_ref, grad_got)
    swap.wait()
    sent = pl.ds(0, size - rows)
    wait_bytes(signal_all.at[sent, :], signal_send)
    wait_bytes(cotangent_all.at[sent, :], cotangent_send)
    wait_bytes(output_all.at[sent, :], output_send)
    wait_bytes(grad_all.at[sent, :], grad_send)
    wait_bytes(grad_part.at[pl.ds(0, n - 1)], filter_send)
    wait_bytes(grad_part.at[pl.ds(0, n - 1)], part_send)


DEPTH = 2


def hand_over_kernel(a_in, b_in, c_in, a_out, b_out, c_out, a_held, b_held, c_held, read, wrote):
    reads, writes = [], []
    for source, target, held in (
        (a_in, a_out, a_held),
        (b_in, b_out, b_held),
        (c_in, c_out, c_held),
    ):
        part = source.shape[0] // DEPTH
        for i in range(DEPTH):
            at, sem = pl.ds(i * part, part), len(reads)
            reads.append(pltpu.make_async_copy(source.at[at], held.at[at], read.at[sem]))
            writes.append(pltpu.make_async_copy(held.at[at], target.at[at], wrote.at[sem]))
    for copy in reads:
        copy.start()
    for before, after in zip(reads, writes):
        before.wait()
        after.start()
    for copy in writes:
        copy.wait()


def whole_body(n, signal, cotangent, filter_spec):
    size = signal.shape[3]
    rows = signal.shape[2]
    half = rows // 2
    tables = [jnp.asarray(table) for table in whole_tables(size)]
    bf16, f32 = jnp.bfloat16, jnp.float32
    anywhere = pl.BlockSpec(memory_space=pl.ANY)
    one_sem = pltpu.SemaphoreType.DMA(())
    three = pltpu.SemaphoreType.DMA((3,))
    landed = pl.pallas_call(
        functools.partial(whole_kernel, n),
        out_shape=tuple(
            jax.ShapeDtypeStruct(x.shape, x.dtype) for x in (signal, cotangent, filter_spec)
        ),
        in_specs=[pl.BlockSpec(memory_space=pltpu.HBM)] * 7,
        out_specs=(anywhere,) * 3,
        scratch_shapes=[
            pltpu.VMEM((size, size), bf16),
            pltpu.VMEM((size, size), bf16),
            pltpu.VMEM((2, n, rows, size), bf16),
            pltpu.VMEM((2 * size, 2 * size), bf16),
            pltpu.VMEM((2 * size, 2 * size), bf16),
            pltpu.VMEM((size, size), f32),
            pltpu.VMEM((size, size), f32),
            pltpu.VMEM((size, 2 * size), f32),
            pltpu.VMEM((size, 2 * size), f32),
            pltpu.VMEM((2 * size, size), bf16),
            pltpu.VMEM((size, size), bf16),
            pltpu.VMEM((size, size), bf16),
            pltpu.VMEM((2, n, rows, size), f32),
            pltpu.VMEM((2, n, half, size), f32),
            pltpu.VMEM((n, half, size), bf16),
            pltpu.VMEM((n, half, size), bf16),
            pltpu.VMEM((n, half, size), bf16),
            pltpu.SemaphoreType.DMA((4,)),
            one_sem,
            one_sem,
            three,
            three,
        ]
        + [one_sem] * 16,
        compiler_params=pltpu.CompilerParams(
            collective_id=0, has_side_effects=True, vmem_limit_bytes=60 * 1024 * 1024
        ),
        cost_estimate=pl.CostEstimate(
            flops=24 * size**3 * 2, bytes_accessed=12 * size * size * 2, transcendentals=0
        ),
    )(signal, cotangent, filter_spec, *tables)
    pieces = 3 * DEPTH
    return pl.pallas_call(
        hand_over_kernel,
        out_shape=tuple(jax.ShapeDtypeStruct(x.shape, x.dtype) for x in landed),
        in_specs=[anywhere] * 3,
        out_specs=(anywhere,) * 3,
        scratch_shapes=[pltpu.VMEM(x.shape, x.dtype) for x in landed]
        + [pltpu.SemaphoreType.DMA((pieces,))] * 2,
        compiler_params=pltpu.CompilerParams(vmem_limit_bytes=60 * 1024 * 1024),
        cost_estimate=pl.CostEstimate(
            flops=0, bytes_accessed=12 * rows * n * size, transcendentals=0
        ),
    )(*landed)


def solution(mesh):
    placed = (P(None, "dp", "seq", None), P(None, "dp", "seq", None), P(None, None, "seq", None))

    def step(signal, cotangent, filter_spec):
        if whole_sequences_fit(mesh, signal, filter_spec):
            return whole_body(mesh.shape["seq"], signal, cotangent, filter_spec)
        return body(signal, cotangent, filter_spec)

    return jax.shard_map(
        step,
        mesh=mesh,
        in_specs=placed,
        out_specs=placed,
        check_vma=False,
    )
```

```python
import functools
import math

import jax
import jax.numpy as jnp
import numpy as np
from jax import lax
from jax.experimental import pallas as pl
from jax.experimental.pallas import tpu as pltpu
from jax.sharding import PartitionSpec as P

MESH = pl.DeviceIdType.MESH

NB = 512


def unit_tables(block_size):
    steps_index = jnp.arange(block_size, dtype=jnp.int32)
    product_index = steps_index[:, None] * steps_index[None, :] % block_size
    phases = product_index.astype(jnp.float32) * (2.0 * math.pi / block_size)
    factor = 1.0 / math.sqrt(block_size)
    return (
        (jnp.cos(phases) * factor).astype(jnp.bfloat16),
        (-jnp.sin(phases) * factor).astype(jnp.bfloat16),
    )


def twiddle(row_index, col_index, length_all, orient):
    phases = (row_index[:, None] * col_index[None, :]).astype(jnp.float32) * (
        orient * 2.0 * math.pi / length_all
    )
    return (jnp.cos(phases), jnp.sin(phases))


def forward_rows(signal, tables, first_row, length_all):
    big_cos, big_sin, small_cos, small_sin = tables
    real_part = jnp.einsum("ncrs,as->ncra", signal, big_cos, preferred_element_type=jnp.float32)
    imaginary = jnp.einsum("ncrs,as->ncra", signal, big_sin, preferred_element_type=jnp.float32)
    row_index = first_row + jnp.arange(signal.shape[2], dtype=jnp.int32)
    col_index = jnp.arange(signal.shape[3], dtype=jnp.int32)
    turn_cos, turn_sin = twiddle(row_index, col_index, length_all, -1.0)
    middle = jnp.stack(
        [real_part * turn_cos - imaginary * turn_sin, real_part * turn_sin + imaginary * turn_cos]
    ).astype(jnp.bfloat16)
    received = lax.all_to_all(middle, "seq", split_axis=4, concat_axis=3, tiled=True)
    real_received = received[0]
    imaginary_received = received[1]
    out_real = jnp.einsum(
        "ncra,qr->ncaq", real_received, small_cos, preferred_element_type=jnp.float32
    ) - jnp.einsum(
        "ncra,qr->ncaq", imaginary_received, small_sin, preferred_element_type=jnp.float32
    )
    out_imaginary = jnp.einsum(
        "ncra,qr->ncaq", imaginary_received, small_cos, preferred_element_type=jnp.float32
    ) + jnp.einsum("ncra,qr->ncaq", real_received, small_sin, preferred_element_type=jnp.float32)
    return jnp.stack([out_real, out_imaginary])


def inverse_rows(spectrum, tables, first_freq, length_all):
    big_cos, big_sin, small_cos, small_sin = tables
    real_part = jnp.einsum(
        "ncaq,rq->ncar", spectrum[0], small_cos, preferred_element_type=jnp.float32
    ) + jnp.einsum("ncaq,rq->ncar", spectrum[1], small_sin, preferred_element_type=jnp.float32)
    imaginary = jnp.einsum(
        "ncaq,rq->ncar", spectrum[1], small_cos, preferred_element_type=jnp.float32
    ) - jnp.einsum("ncaq,rq->ncar", spectrum[0], small_sin, preferred_element_type=jnp.float32)
    row_index = first_freq + jnp.arange(spectrum.shape[3], dtype=jnp.int32)
    col_index = jnp.arange(spectrum.shape[4], dtype=jnp.int32)
    turn_cos, turn_sin = twiddle(row_index, col_index, length_all, 1.0)
    middle = jnp.stack(
        [real_part * turn_cos - imaginary * turn_sin, real_part * turn_sin + imaginary * turn_cos]
    ).astype(jnp.bfloat16)
    received = lax.all_to_all(middle, "seq", split_axis=4, concat_axis=3, tiled=True)
    total = jnp.einsum(
        "ncar,sa->ncrs", received[0], big_cos, preferred_element_type=jnp.float32
    ) + jnp.einsum("ncar,sa->ncrs", received[1], big_sin, preferred_element_type=jnp.float32)
    return total.astype(jnp.bfloat16)


def body(signal, cotangent, filter_spec):
    rows_total = signal.shape[2] * lax.axis_size("seq")
    big_cos, big_sin = unit_tables(NB)
    small_cos, small_sin = unit_tables(rows_total)
    tables = (big_cos, big_sin, small_cos, small_sin)
    length_all = NB * rows_total
    first_row = lax.axis_index("seq") * signal.shape[2]
    first_freq = lax.axis_index("seq") * (NB // lax.axis_size("seq"))
    filter_real = filter_spec[0].astype(jnp.float32)[:, None]
    filter_imaginary = filter_spec[1].astype(jnp.float32)[:, None]
    channels = signal.shape[1]
    stacked = forward_rows(
        jnp.concatenate([signal, cotangent], axis=1), tables, first_row, length_all
    )
    signal_spec = stacked[:, :, :channels]
    cotangent_spec = stacked[:, :, channels:]
    joined_input = jnp.concatenate(
        [
            jnp.stack(
                [
                    filter_real * signal_spec[0] - filter_imaginary * signal_spec[1],
                    filter_real * signal_spec[1] + filter_imaginary * signal_spec[0],
                ]
            ).astype(jnp.bfloat16),
            jnp.stack(
                [
                    filter_real * cotangent_spec[0] + filter_imaginary * cotangent_spec[1],
                    filter_real * cotangent_spec[1] - filter_imaginary * cotangent_spec[0],
                ]
            ).astype(jnp.bfloat16),
        ],
        axis=2,
    )
    results = inverse_rows(joined_input, tables, first_freq, length_all)
    output = results[:, :channels]
    grad_signal = results[:, channels:]
    grad_terms = jnp.stack(
        [
            jnp.sum(
                cotangent_spec[0] * signal_spec[0] + cotangent_spec[1] * signal_spec[1], axis=1
            ),
            jnp.sum(
                cotangent_spec[1] * signal_spec[0] - cotangent_spec[0] * signal_spec[1], axis=1
            ),
        ]
    )
    grad_filter = lax.psum(grad_terms, "dp")
    return (output, grad_signal, grad_filter.astype(jnp.bfloat16))


def whole_tables(size):
    index = np.arange(size)
    phases = (index[:, None] * index[None, :] % size) * (2.0 * math.pi / size)
    factor = 1.0 / math.sqrt(size)
    cos_table, sin_table = np.cos(phases) * factor, -np.sin(phases) * factor
    forward = np.block([[cos_table, sin_table], [-sin_table, cos_table]])
    turn = (index[:, None] * index[None, :]) * (2.0 * math.pi / (size * size))
    return (
        forward.astype(jnp.bfloat16),
        forward.T.astype(jnp.bfloat16),
        np.cos(turn).astype(np.float32),
        np.sin(turn).astype(np.float32),
    )


def whole_sequences_fit(mesh, signal, filter_spec):
    filters, channels, rows, size = signal.shape
    n = mesh.shape["seq"]
    return (
        mesh.shape["dp"] == 2
        and channels == 2
        and filters * channels == n
        and rows * n == size
        and filter_spec.shape[2] == rows
        and filter_spec.shape[3] == size
        and rows % 32 == 0
        and size % 256 == 0
    )


def whole_kernel(
    n,
    signal_ref,
    cotangent_ref,
    filter_ref,
    forward_ref,
    inverse_ref,
    cos_ref,
    sin_ref,
    output_ref,
    grad_signal_ref,
    grad_filter_ref,
    signal_all,
    cotangent_all,
    filter_all,
    forward_table,
    inverse_table,
    turn_cos,
    turn_sin,
    signal_spec,
    cotangent_spec,
    middle,
    output_all,
    grad_all,
    terms_wide,
    terms_mate,
    terms_out,
    terms_got,
    grad_part,
    table_sem,
    filter_send,
    filter_got,
    share_send,
    share_got,
    signal_send,
    signal_got,
    cotangent_send,
    cotangent_got,
    output_send,
    output_got,
    grad_send,
    grad_got,
    mate_send,
    mate_got,
    terms_send,
    terms_recv,
    part_send,
    part_got,
    swap_send,
    swap_got,
):
    size = signal_all.shape[0]
    rows = size // n
    half = rows // 2
    chunk = 256
    chunks = size // chunk
    per_chunk = chunk // rows
    me = lax.axis_index("seq")
    side = lax.axis_index("dp")
    other = 1 - side
    channel = lax.rem(me, 2)
    group = lax.div(me, 2)
    mate = me + 1 - 2 * channel
    my_half = pl.ds(pl.multiple_of(channel * half, half), half)
    my_rows = pl.ds(pl.multiple_of(me * rows, rows), rows)
    partners = ((side, mate), (other, me), (other, mate))

    table_copies = [
        pltpu.make_async_copy(source, target, table_sem.at[i])
        for i, (source, target) in enumerate(
            (
                (forward_ref, forward_table),
                (inverse_ref, inverse_table),
                (cos_ref, turn_cos),
                (sin_ref, turn_sin),
            )
        )
    ]
    for copy in table_copies:
        copy.start()

    barrier = pltpu.get_barrier_semaphore()

    def greet(k, carry):
        pl.semaphore_signal(
            barrier, inc=1, device_id={"dp": side, "seq": lax.rem(me + k, n)}, device_id_type=MESH
        )
        return carry

    lax.fori_loop(1, n, greet, 0)
    for to_side, to_seq in partners[1:]:
        pl.semaphore_signal(
            barrier, inc=1, device_id={"dp": to_side, "seq": to_seq}, device_id_type=MESH
        )
    pl.semaphore_wait(barrier, n + 1)

    across = n // 2
    my_part, place = lax.div(me, across), lax.rem(me, across)

    def for_peers(first, last, send):
        if first == 1:
            send((1 - my_part) * across + place)

        def one(t, carry):
            part = lax.rem(my_part + lax.rem(t + me, 2), 2)
            send(part * across + lax.rem(place + lax.div(t, 2), across))
            return carry

        lax.fori_loop(max(first, 2), last, one, 0)

    def send_all(source_of, target, send_sem, recv_sem, first=1, last=n):
        if first == 1:
            pltpu.make_async_copy(source_of(me), target, recv_sem).start()

        def send(to):
            pltpu.make_async_remote_copy(
                src_ref=source_of(to),
                dst_ref=target,
                send_sem=send_sem,
                recv_sem=recv_sem,
                device_id={"dp": side, "seq": to},
                device_id_type=MESH,
            ).start()

        for_peers(first, last, send)

    def wait_bytes(ref, sem):
        pltpu.make_async_copy(ref, ref, sem).wait()

    def filter_source(to):
        start = pl.multiple_of(lax.rem(to, 2) * half, half)
        return filter_ref.at[side, lax.div(to, 2), pl.ds(start, half), :]

    pltpu.make_async_copy(
        filter_source(me), filter_all.at[side, me, my_half, :], filter_got
    ).start()

    def send_filter(to):
        start = pl.multiple_of(lax.rem(to, 2) * half, half)
        pltpu.make_async_remote_copy(
            src_ref=filter_source(to),
            dst_ref=filter_all.at[side, me, pl.ds(start, half), :],
            send_sem=filter_send,
            recv_sem=filter_got,
            device_id={"dp": side, "seq": to},
            device_id_type=MESH,
        ).start()

    for_peers(1, n, send_filter)
    send_all(
        lambda to: signal_ref.at[lax.div(to, 2), lax.rem(to, 2)],
        signal_all.at[my_rows, :],
        signal_send,
        signal_got,
    )

    my_quarter = filter_all.at[side, :, my_half, :]
    wait_bytes(my_quarter, filter_got)
    other_quarter = filter_all.at[other, :, my_half, :]
    share_copies = [
        pltpu.make_async_remote_copy(
            src_ref=quarter,
            dst_ref=quarter,
            send_sem=share_send.at[i],
            recv_sem=share_got.at[i],
            device_id={"dp": to_side, "seq": to_seq},
            device_id_type=MESH,
        )
        for i, (quarter, to_side, to_seq) in enumerate(
            (
                (my_quarter, other, me),
                (my_quarter, side, mate),
                (other_quarter, side, mate),
            )
        )
    ]
    share_copies[0].start()
    share_copies[1].start()
    send_all(
        lambda to: cotangent_ref.at[lax.div(to, 2), lax.rem(to, 2)],
        cotangent_all.at[my_rows, :],
        cotangent_send,
        cotangent_got,
    )
    share_copies[0].wait_recv()
    share_copies[2].start()

    for copy in table_copies:
        copy.wait()

    def transform(values, spec, i):
        at = pl.ds(pl.multiple_of(i * chunk, chunk), chunk)
        one_signal = values[...]
        contract_last = (((1,), (1,)), ((), ()))
        real = lax.dot_general(
            forward_table[at, :size], one_signal, contract_last, preferred_element_type=jnp.float32
        )
        imaginary = lax.dot_general(
            forward_table[at, size:], one_signal, contract_last, preferred_element_type=jnp.float32
        )
        cos_part, sin_part = turn_cos[at, :], turn_sin[at, :]
        mid = jnp.concatenate(
            [
                (real * cos_part + imaginary * sin_part).astype(jnp.bfloat16),
                (imaginary * cos_part - real * sin_part).astype(jnp.bfloat16),
            ],
            axis=1,
        )
        spec[at, :] = jnp.dot(mid, forward_table[...], preferred_element_type=jnp.float32)

    def filtered(spec, sign, i):
        at = pl.ds(pl.multiple_of(i * chunk, chunk), chunk)
        blocks = pl.ds(i * per_chunk, per_chunk)
        filter_real = filter_all[0, blocks].reshape(chunk, size).astype(jnp.float32)
        filter_imaginary = filter_all[1, blocks].reshape(chunk, size).astype(jnp.float32) * sign
        real, imaginary = spec[at, :size], spec[at, size:]
        product = jnp.concatenate(
            [
                (filter_real * real - filter_imaginary * imaginary).astype(jnp.bfloat16),
                (filter_real * imaginary + filter_imaginary * real).astype(jnp.bfloat16),
            ],
            axis=1,
        )
        both = jnp.dot(product, inverse_table[...], preferred_element_type=jnp.float32)
        real, imaginary = both[:, :size], both[:, size:]
        cos_part, sin_part = turn_cos[at, :], turn_sin[at, :]
        middle[at, :] = (real * cos_part - imaginary * sin_part).astype(jnp.bfloat16)
        below = pl.ds(pl.multiple_of(size + i * chunk, chunk), chunk)
        middle[below, :] = (real * sin_part + imaginary * cos_part).astype(jnp.bfloat16)

    def restored(result, i):
        at = pl.ds(pl.multiple_of(i * chunk, chunk), chunk)
        turned = jnp.dot(
            forward_table[at, :], middle[...], preferred_element_type=jnp.float32
        )
        result[:, at] = turned.T.astype(jnp.bfloat16)

    def loop(fn):
        for i in range(chunks):
            fn(i)

    def rows_of(ref, to):
        return ref.at[pl.ds(pl.multiple_of(to * rows, rows), rows), :]

    wait_bytes(signal_all, signal_got)
    loop(lambda i: transform(signal_all, signal_spec, i))
    share_copies[0].wait_send()
    share_copies[1].wait()
    share_copies[2].wait()
    loop(lambda i: filtered(signal_spec, 1.0, i))
    loop(lambda i: restored(output_all, i))
    send_all(
        lambda to: rows_of(output_all, to), output_ref.at[group, channel], output_send, output_got
    )

    wait_bytes(cotangent_all, cotangent_got)

    def transform_and_terms(i):
        transform(cotangent_all, cotangent_spec, i)
        at = pl.ds(pl.multiple_of(i * chunk, chunk), chunk)
        blocks = pl.ds(i * per_chunk, per_chunk)
        real, imaginary = signal_spec[at, :size], signal_spec[at, size:]
        back_real, back_imaginary = cotangent_spec[at, :size], cotangent_spec[at, size:]
        for part, values in enumerate(
            (
                back_real * real + back_imaginary * imaginary,
                back_imaginary * real - back_real * imaginary,
            )
        ):
            terms_wide[part, blocks] = values.reshape(per_chunk, rows, size)

    loop(transform_and_terms)
    mate_half = pl.ds(pl.multiple_of(half - channel * half, half), half)
    mate_copy = pltpu.make_async_remote_copy(
        src_ref=terms_wide.at[:, :, mate_half, :],
        dst_ref=terms_mate,
        send_sem=mate_send,
        recv_sem=mate_got,
        device_id={"dp": side, "seq": mate},
        device_id_type=MESH,
    )
    mate_copy.start()

    loop(lambda i: filtered(cotangent_spec, -1.0, i))
    mate_copy.wait()
    terms_out[...] = (terms_wide[other, :, my_half, :] + terms_mate[other]).astype(jnp.bfloat16)
    terms_copy = pltpu.make_async_remote_copy(
        src_ref=terms_out,
        dst_ref=terms_got,
        send_sem=terms_send,
        recv_sem=terms_recv,
        device_id={"dp": other, "seq": me},
        device_id_type=MESH,
    )
    terms_copy.start()
    loop(lambda i: restored(grad_all, i))
    send_grad = functools.partial(
        send_all,
        lambda to: rows_of(grad_all, to),
        grad_signal_ref.at[group, channel],
        grad_send,
        grad_got,
    )
    send_grad(1, across)

    terms_copy.wait()
    grad_part[...] = (
        terms_wide[side, :, my_half, :] + terms_mate[side] + terms_got[...].astype(jnp.float32)
    ).astype(jnp.bfloat16)
    send_all(
        lambda to: grad_part.at[to],
        grad_filter_ref.at[side, group, my_half, :],
        part_send,
        part_got,
    )
    send_grad(across, n)
    wait_bytes(grad_filter_ref.at[side], part_got)
    swap = pltpu.make_async_remote_copy(
        src_ref=grad_filter_ref.at[side],
        dst_ref=grad_filter_ref.at[side],
        send_sem=swap_send,
        recv_sem=swap_got,
        device_id={"dp": other, "seq": me},
        device_id_type=MESH,
    )
    swap.start()

    wait_bytes(output_ref, output_got)
    wait_bytes(grad_signal_ref, grad_got)
    swap.wait()
    sent = pl.ds(0, size - rows)
    wait_bytes(signal_all.at[sent, :], signal_send)
    wait_bytes(cotangent_all.at[sent, :], cotangent_send)
    wait_bytes(output_all.at[sent, :], output_send)
    wait_bytes(grad_all.at[sent, :], grad_send)
    wait_bytes(grad_part.at[pl.ds(0, n - 1)], filter_send)
    wait_bytes(grad_part.at[pl.ds(0, n - 1)], part_send)


DEPTH = 2


def hand_over_kernel(a_in, b_in, c_in, a_out, b_out, c_out, a_held, b_held, c_held, read, wrote):
    reads, writes = [], []
    for source, target, held in (
        (a_in, a_out, a_held),
        (b_in, b_out, b_held),
        (c_in, c_out, c_held),
    ):
        part = source.shape[0] // DEPTH
        for i in range(DEPTH):
            at, sem = pl.ds(i * part, part), len(reads)
            reads.append(pltpu.make_async_copy(source.at[at], held.at[at], read.at[sem]))
            writes.append(pltpu.make_async_copy(held.at[at], target.at[at], wrote.at[sem]))
    for copy in reads:
        copy.start()
    for before, after in zip(reads, writes):
        before.wait()
        after.start()
    for copy in writes:
        copy.wait()


def whole_body(n, signal, cotangent, filter_spec):
    size = signal.shape[3]
    rows = signal.shape[2]
    half = rows // 2
    tables = [jnp.asarray(table) for table in whole_tables(size)]
    bf16, f32 = jnp.bfloat16, jnp.float32
    anywhere = pl.BlockSpec(memory_space=pl.ANY)
    one_sem = pltpu.SemaphoreType.DMA(())
    three = pltpu.SemaphoreType.DMA((3,))
    landed = pl.pallas_call(
        functools.partial(whole_kernel, n),
        out_shape=tuple(
            jax.ShapeDtypeStruct(x.shape, x.dtype) for x in (signal, cotangent, filter_spec)
        ),
        in_specs=[pl.BlockSpec(memory_space=pltpu.HBM)] * 7,
        out_specs=(anywhere,) * 3,
        scratch_shapes=[
            pltpu.VMEM((size, size), bf16),
            pltpu.VMEM((size, size), bf16),
            pltpu.VMEM((2, n, rows, size), bf16),
            pltpu.VMEM((2 * size, 2 * size), bf16),
            pltpu.VMEM((2 * size, 2 * size), bf16),
            pltpu.VMEM((size, size), f32),
            pltpu.VMEM((size, size), f32),
            pltpu.VMEM((size, 2 * size), f32),
            pltpu.VMEM((size, 2 * size), f32),
            pltpu.VMEM((2 * size, size), bf16),
            pltpu.VMEM((size, size), bf16),
            pltpu.VMEM((size, size), bf16),
            pltpu.VMEM((2, n, rows, size), f32),
            pltpu.VMEM((2, n, half, size), f32),
            pltpu.VMEM((n, half, size), bf16),
            pltpu.VMEM((n, half, size), bf16),
            pltpu.VMEM((n, half, size), bf16),
            pltpu.SemaphoreType.DMA((4,)),
            one_sem,
            one_sem,
            three,
            three,
        ]
        + [one_sem] * 16,
        compiler_params=pltpu.CompilerParams(
            collective_id=0, has_side_effects=True, vmem_limit_bytes=60 * 1024 * 1024
        ),
        cost_estimate=pl.CostEstimate(
            flops=24 * size**3 * 2, bytes_accessed=12 * size * size * 2, transcendentals=0
        ),
    )(signal, cotangent, filter_spec, *tables)
    pieces = 3 * DEPTH
    return pl.pallas_call(
        hand_over_kernel,
        out_shape=tuple(jax.ShapeDtypeStruct(x.shape, x.dtype) for x in landed),
        in_specs=[anywhere] * 3,
        out_specs=(anywhere,) * 3,
        scratch_shapes=[pltpu.VMEM(x.shape, x.dtype) for x in landed]
        + [pltpu.SemaphoreType.DMA((pieces,))] * 2,
        compiler_params=pltpu.CompilerParams(vmem_limit_bytes=60 * 1024 * 1024),
        cost_estimate=pl.CostEstimate(
            flops=0, bytes_accessed=12 * rows * n * size, transcendentals=0
        ),
    )(*landed)


def solution(mesh):
    placed = (P(None, "dp", "seq", None), P(None, "dp", "seq", None), P(None, None, "seq", None))

    def step(signal, cotangent, filter_spec):
        if whole_sequences_fit(mesh, signal, filter_spec):
            return whole_body(mesh.shape["seq"], signal, cotangent, filter_spec)
        return body(signal, cotangent, filter_spec)

    return jax.shard_map(
        step,
        mesh=mesh,
        in_specs=placed,
        out_specs=placed,
        check_vma=False,
    )
```
